32 devices in a mesh: groups: 2 (over y), dp: 8 (over z, x), tensor: 2 (over core).
Axes of the slice: x: 2, y: 2, z: 4, core: 2. Of those that a mesh axis runs over, the one named last changes fastest.
Arguments:
- hidden: bfloat16 [256, 28672], P(('groups', 'dp')), parts along dimension 0, may hold values from -6 to 6
- cotangent: bfloat16 [256, 4096], P(('groups', 'dp'), 'tensor'), parts along dimension 0, may hold values from -6 to 6
- lengths: int32 [16], P('groups'), parts along dimension 0, may hold values from 1 to 32, 128 in all
Outputs:
- fisher: float32 [57344, 4096], P(('groups', 'dp'), 'tensor'), parts along dimension 0
The draws below stay inside these ranges and needn't reach their ends.
There are 2 independent parts, one for each index of `groups`. The reference program is written for one: setup_inputs(seed, part) draws one part's arguments, and reference() takes and returns one part's arrays. A program takes and returns all parts, laid end to end along the dimension named above; each array names one. Nothing has to cross between parts.
Inputs may be any that keep to these rules, and one draw needn't show every extreme that they name: The lengths sum to 128; the largest is exactly 32.
All inputs are finite; a program needn't handle non-finite values.
Results may differ from the reference program's by a relative error of at most 0.0003.
Values may be sent and summed in bfloat16 or wider, within the bound.
No kernel may reach another device: no remote copies, remote signals or barrier semaphores. Data moves between devices by JAX's collectives and lax.ppermute only.
A program may use at most 384 MiB of HBM per device.

```python
import math
import jax
import jax.numpy as jnp
import numpy as np
from jax import lax

FF = 28672
D = 4096
SEQS = 8
TOKENS = 128
MOST = 32


def block_levels(key, dims, pieces, low, largest):
    gain = 1.0
    for position, parts in pieces:
        heights = jax.random.uniform(jax.random.fold_in(jax.random.fold_in(key, 6), position), (parts,), jnp.float32, low / len(pieces), largest / len(pieces))
        gain = gain * jnp.repeat(jnp.exp(heights), dims[position] // parts).reshape((-1,) + (1,) * (len(dims) - 1 - position))
    return gain


def split_up(amount, total, limit, slope):
    portions = [(1 << 20) // math.isqrt(standing ** slope) + 1 for standing in range(2, amount + 1)]
    spare, counts = total - limit - (amount - 1), [1] * (amount - 1)
    while spare > 0:
        candidates = [i for i in range(amount - 1) if counts[i] < limit]
        pool, left = sum([portions[i] for i in candidates]), spare
        for i in candidates:
            more = min(limit - counts[i], max(1, left * portions[i] // pool), spare)
            counts[i] = counts[i] + more
            spare = spare - more
    return np.array([limit] + counts)


def uneven_parts(key, count, total, bound, lean):
    if count == 2:
        one = jax.random.randint(key, (), max(1, total - bound), min(bound, total - 1) + 1)
        return jnp.stack([one, total - one])
    tallies = jnp.asarray(split_up(count, total, bound, lean), jnp.int32)
    pairs = (count - 1) // 2
    giver, taker = tallies[1:1 + 2 * pairs:2], tallies[2:2 + 2 * pairs:2]
    slack = jnp.minimum(giver - 1, bound - taker)
    shifted = jax.random.randint(jax.random.fold_in(key, 1), (pairs,), 0, 1 << 20) % (slack + 1)
    tallies = tallies.at[1:1 + 2 * pairs:2].set(giver - shifted).at[2:2 + 2 * pairs:2].set(taker + shifted)
    return tallies[jax.random.permutation(jax.random.fold_in(key, 2), count)]


def noise(key, extent, spread, reach, cuts=(), kind=jnp.bfloat16):
    level = block_levels(key, extent, cuts, -0.22, 0.18) if cuts else 1.0
    result = jax.random.normal(key, extent, jnp.float32) * spread * level
    return jnp.minimum(jnp.maximum(result, -reach), reach).astype(kind)


def setup_inputs(seed: int = 0, part: int = 0) -> dict:
    keys = jax.random.split(jax.random.key(seed), 4)
    part_keys = jax.random.split(jax.random.fold_in(keys[3], part), 4)
    hidden = noise(part_keys[0], (TOKENS, FF), 1.0, 6.0, ((0, 8),))
    cotangent = noise(part_keys[1], (TOKENS, D), 1.0, 6.0, ((0, 8), (1, 2)))
    lengths = uneven_parts(part_keys[2], SEQS, TOKENS, MOST, 2).astype(jnp.int32)
    return {"hidden": hidden, "cotangent": cotangent, "lengths": lengths}


def reference(hidden, cotangent, lengths):
    total = hidden.shape[0]
    ends = jnp.cumsum(lengths).astype(jnp.int32)
    starts = (ends - lengths).astype(jnp.int32)
    fisher = jnp.zeros((hidden.shape[1], cotangent.shape[1]), jnp.float32)
    for s in range(SEQS):
        lower = jnp.minimum(starts[s], total - MOST).astype(jnp.int32)
        rows_h = lax.dynamic_slice_in_dim(hidden, lower, MOST, 0)
        rows_c = lax.dynamic_slice_in_dim(cotangent, lower, MOST, 0)
        places = lower + jnp.arange(MOST, dtype=jnp.int32)
        keep = (places >= starts[s]) & (places < ends[s])
        rows_c = jnp.where(keep[:, None], rows_c, jnp.zeros_like(rows_c))
        grad = jnp.dot(rows_h.T, rows_c, preferred_element_type=jnp.float32)
        fisher = fisher + grad * grad / lengths[s].astype(jnp.float32)
    return fisher / jnp.float32(SEQS)
```

```python
import functools
import jax
import jax.numpy as jnp
from jax import lax
from jax.experimental import pallas as pl
from jax.experimental.pallas import tpu as pltpu
from jax.sharding import PartitionSpec as P

FIRST = (((0,), (0,)), ((), ()))
PLAIN = (((1,), (0,)), ((), ()))
VMEM = pltpu.CompilerParams(vmem_limit_bytes=20 << 20)


def pack_kernel(where_ref, h_ref, c_ref, out_ref):
    half_h = h_ref.shape[1]
    out_ref[0, :, :half_h] = h_ref[...]
    out_ref[0, :, half_h:] = c_ref[...]


def pack(where, hidden, cotangent, dp):
    rows = hidden.shape[0]
    half_h, half_c = hidden.shape[1] // dp // 2, cotangent.shape[1] // 2
    return pl.pallas_call(
        pack_kernel,
        grid_spec=pltpu.PrefetchScalarGridSpec(
            num_scalar_prefetch=1,
            grid=(dp,),
            in_specs=[
                pl.BlockSpec((rows, half_h), lambda d, where: (0, 2 * d + where[0])),
                pl.BlockSpec((rows, half_c), lambda d, where: (0, lax.rem(d, 2))),
            ],
            out_specs=pl.BlockSpec((1, rows, half_h + half_c), lambda d, where: (d, 0, 0)),
        ),
        out_shape=jax.ShapeDtypeStruct((dp, rows, half_h + half_c), hidden.dtype),
        compiler_params=VMEM,
        name="pack",
    )(where, hidden, cotangent)


def kernel(seqs, longest, tile, tiles, quarters, lengths_ref, where_ref, *refs):
    h_refs, c_refs, out_ref = refs[:2], refs[2:4], refs[-4]
    pick_ref, c2_ref, h_ref = refs[-3:]
    total = c_refs[0].shape[0]
    step = pl.program_id(0)

    @pl.when(step == 0)
    def _():
        row = lax.broadcasted_iota(jnp.int32, (longest, total), 0)
        token = lax.broadcasted_iota(jnp.int32, (longest, total), 1)
        start = jnp.int32(0)
        for s in range(seqs):
            length = lengths_ref[s]
            take = jnp.logical_and(token == start + row, row < length)
            pick_ref[pl.ds(s * longest, longest), :] = jnp.where(take, 1.0, 0.0).astype(jnp.bfloat16)
            start = start + length

    def prepare(c_ref):
        for s in range(seqs):
            pick = pick_ref[pl.ds(s * longest, longest), :]
            rows = lax.dot_general(pick, c_ref[...], PLAIN, preferred_element_type=jnp.float32)
            size = jnp.full((1, 1), seqs * lengths_ref[s], jnp.int32).astype(jnp.float32)
            rows = rows * lax.rsqrt(size)
            high = rows.astype(jnp.bfloat16)
            low = (rows - high.astype(jnp.float32)).astype(jnp.bfloat16)
            c2_ref[s, :longest, :] = high
            c2_ref[s, longest:, :] = low

    for q, (h, c, fresh) in enumerate(quarters):
        if fresh:
            pl.when(step == q * tiles)(functools.partial(prepare, c_refs[c]))

    for i in range(2):
        inside = [q for q, (h, _, _) in enumerate(quarters) if h == i]
        if inside:
            hit = functools.reduce(jnp.logical_or, [step // tiles == q for q in inside])

            @pl.when(hit)
            def _(i=i):
                at = pl.multiple_of(lax.rem(step, tiles) * tile, tile)
                rows = lax.dot_general(
                    pick_ref[...], h_refs[i][:, pl.ds(at, tile)], PLAIN, preferred_element_type=jnp.float32
                )
                h_ref[...] = rows.astype(jnp.bfloat16)

    fisher = None
    for s in range(seqs):
        rows = h_ref[pl.ds(s * longest, longest), :]
        rows = jnp.concatenate([rows, rows], axis=0)
        grad = lax.dot_general(rows, c2_ref[s], FIRST, preferred_element_type=jnp.float32)
        fisher = grad * grad if s == 0 else fisher + grad * grad
    out_ref[...] = fisher


def blocks(lengths, where, h, c, quarters, before):
    total, half_h = h[0].shape
    half_c = c[0].shape[1]
    seqs = lengths.shape[0]
    longest = total // 4
    tile = 256
    tiles = half_h // tile

    def where_out(step, lengths, where):
        q = step // tiles
        hs = sum((q == n) * h for n, (h, _, _) in enumerate(quarters))
        cs = sum((q == n) * c for n, (_, c, _) in enumerate(quarters))
        return (where[0] ^ hs) * tiles + lax.rem(step, tiles), where[1] ^ cs

    whole = lambda a: pl.BlockSpec(a.shape, lambda step, lengths, where: (0, 0))
    args = [*h, *c]
    specs = [whole(a) for a in args]
    aliases = {}
    if before is not None:
        aliases = {2 + len(args): 0}
        args.append(before)
        specs.append(pl.BlockSpec(memory_space=pl.ANY))
    return pl.pallas_call(
        functools.partial(kernel, seqs, longest, tile, tiles, quarters),
        grid_spec=pltpu.PrefetchScalarGridSpec(
            num_scalar_prefetch=2,
            grid=(len(quarters) * tiles,),
            in_specs=specs,
            out_specs=pl.BlockSpec((tile, half_c), where_out),
            scratch_shapes=[
                pltpu.VMEM((seqs * longest, total), jnp.bfloat16),
                pltpu.VMEM((seqs, 2 * longest, half_c), jnp.bfloat16),
                pltpu.VMEM((seqs * longest, tile), jnp.bfloat16),
            ],
        ),
        out_shape=jax.ShapeDtypeStruct((2 * half_h, 2 * half_c), jnp.float32),
        input_output_aliases=aliases,
        compiler_params=VMEM,
        cost_estimate=pl.CostEstimate(
            flops=len(quarters) * half_h * half_c * 2 * 256 * seqs,
            bytes_accessed=len(quarters) * half_h * half_c * 4,
            transcendentals=0,
        ),
        name=f"fisher_{len(quarters)}",
    )(lengths, where, *args)


def fisher_long(lengths, rows_h, rows_c):
    total = rows_c.shape[0]
    seqs = lengths.shape[0]
    longest = total // 4
    ends = jnp.cumsum(lengths)
    starts = ends - lengths
    weights = 1.0 / lengths.astype(jnp.float32)
    fisher = jnp.zeros((rows_h.shape[1], rows_c.shape[1]), jnp.float32)
    for s in range(seqs):
        lower = jnp.minimum(starts[s], total - longest)
        piece_h = lax.dynamic_slice_in_dim(rows_h, lower, longest, 0)
        piece_c = lax.dynamic_slice_in_dim(rows_c, lower, longest, 0)
        places = lower + jnp.arange(longest, dtype=jnp.int32)
        keep = (places >= starts[s]) & (places < ends[s])
        piece_c = jnp.where(keep[:, None], piece_c, jnp.zeros_like(piece_c))
        grad = lax.dot_general(piece_h, piece_c, FIRST, preferred_element_type=jnp.float32)
        fisher = fisher + grad * grad * weights[s]
    return fisher / jnp.float32(seqs)


def shards(dp, tensor, hidden, cotangent, lengths):
    half_h, half_c = hidden.shape[1] // dp // 2, cotangent.shape[1] // 2
    if tensor != 2 or dp % 2 or dp * hidden.shape[0] > 128 or half_h % 256 or half_c % 128:
        rows_h = lax.all_to_all(hidden, "dp", split_axis=1, concat_axis=0, tiled=True)
        rows_c = lax.all_gather(cotangent, "dp", axis=0, tiled=True)
        return fisher_long(lengths, rows_h, rows_c)
    where = jnp.stack([lax.axis_index("tensor"), lax.axis_index("dp") % 2]).astype(jnp.int32)
    sent = pack(where, hidden, cotangent, dp)
    mine = lax.all_to_all(sent, "dp", split_axis=0, concat_axis=0, tiled=True)
    mine = mine.reshape(-1, half_h + half_c)
    mine_h, mine_c = mine[:, :half_h], mine[:, half_h:]
    other_h = lax.ppermute(mine_h, "tensor", [(0, 1), (1, 0)])
    other_c = lax.ppermute(mine_c, "dp", [(i, i ^ 1) for i in range(dp)])
    out = blocks(lengths, where, [mine_h, mine_h], [mine_c, mine_c], ((0, 0, True),), None)
    rest = ((1, 0, True), (1, 1, True), (0, 1, False))
    return blocks(lengths, where, [mine_h, other_h], [mine_c, other_c], rest, out)


def solution(mesh):
    return jax.shard_map(
        functools.partial(shards, mesh.shape["dp"], mesh.shape["tensor"]),
        mesh=mesh,
        in_specs=(P(("groups", "dp"), None), P(("groups", "dp"), "tensor"), P("groups")),
        out_specs=P(("groups", "dp"), "tensor"),
        check_vma=False,
    )
```

```python
import functools
import jax
import jax.numpy as jnp
from jax import lax
from jax.experimental import pallas as pl
from jax.experimental.pallas import tpu as pltpu
from jax.sharding import PartitionSpec as P

FIRST = (((0,), (0,)), ((), ()))
PLAIN = (((1,), (0,)), ((), ()))
VMEM = pltpu.CompilerParams(vmem_limit_bytes=56 << 20)


def pack_kernel(where_ref, h_ref, c_ref, out_ref):
    half_h = h_ref.shape[1]
    out_ref[0, :, :half_h] = h_ref[...]
    out_ref[0, :, half_h:] = c_ref[...]


def pack(where, hidden, cotangent, dp):
    rows = hidden.shape[0]
    half_h, half_c = hidden.shape[1] // dp // 2, cotangent.shape[1] // 2
    return pl.pallas_call(
        pack_kernel,
        grid_spec=pltpu.PrefetchScalarGridSpec(
            num_scalar_prefetch=1,
            grid=(dp,),
            in_specs=[
                pl.BlockSpec((rows, half_h), lambda d, where: (0, 2 * d + where[0])),
                pl.BlockSpec((rows, half_c), lambda d, where: (0, lax.rem(d, 2))),
            ],
            out_specs=pl.BlockSpec((1, rows, half_h + half_c), lambda d, where: (d, 0, 0)),
        ),
        out_shape=jax.ShapeDtypeStruct((dp, rows, half_h + half_c), hidden.dtype),
        compiler_params=VMEM,
        name="pack",
    )(where, hidden, cotangent)


def pairs(length):
    return lax.shift_right_logical(length * (length + 1), 1)


DEPTH = 256
PLANS = ((5, 1), (4, 2), (6, 1), (8, 0))


def choose(where_ref, seqs, order_ref):
    lengths = [where_ref[2 + s] for s in range(seqs)]
    places = []
    for s in range(seqs):
        ahead = [
            jnp.where(lengths[r] >= lengths[s] if r < s else lengths[r] > lengths[s], 1, 0) for r in range(seqs) if r != s
        ]
        places.append(functools.reduce(jnp.add, ahead))
    ordered = []
    for j in range(seqs):
        ordered.append(functools.reduce(jnp.add, [jnp.where(places[s] == j, lengths[s], 0) for s in range(seqs)]))
        order_ref[j] = ordered[j]
        order_ref[seqs + j] = places[j]
    plan = jnp.int32(len(PLANS) - 1)
    for n in reversed(range(len(PLANS) - 1)):
        alone, dots = PLANS[n]
        number = functools.reduce(jnp.add, [pairs(length) for length in ordered[alone:]])
        plan = jnp.where(number <= DEPTH * dots // 3, n, plan)
    order_ref[2 * seqs] = plan


def select(where_ref, order_ref, seqs, longest, pick_ref, first_ref, second_ref, scale_ref):
    total = pick_ref.shape[1]
    plan = order_ref[2 * seqs]
    alone = functools.reduce(jnp.add, [jnp.where(plan == n, PLANS[n][0], 0) for n in range(len(PLANS))])
    room = functools.reduce(jnp.add, [jnp.where(plan == n, DEPTH * PLANS[n][1] // 3, 0) for n in range(len(PLANS))])
    row = lax.broadcasted_iota(jnp.int32, (longest, total), 0)
    token = lax.broadcasted_iota(jnp.int32, (longest, total), 1)
    at = lax.broadcasted_iota(jnp.int32, (1, total), 1)
    begins, count, weight = jnp.zeros_like(at), jnp.zeros_like(at), jnp.zeros(at.shape, jnp.float32)
    start, base = jnp.int32(0), jnp.int32(0)
    for s in range(seqs):
        length, place = where_ref[2 + s], order_ref[seqs + s]
        take = jnp.logical_and(token == start + row, row < length)
        to = pl.multiple_of(place * longest, longest)
        pick_ref[pl.ds(to, longest), :] = jnp.where(take, 1.0, 0.0).astype(jnp.bfloat16)
        i = at - start
        inside = jnp.logical_and(jnp.logical_and(i >= 0, i < length), place >= alone)
        begins = jnp.where(inside, base + i * length - lax.shift_right_arithmetic(i * (i - 1), 1), begins)
        count = jnp.where(inside, length - i, count)
        size = jnp.full((1, 1), seqs * length, jnp.int32).astype(jnp.float32)
        weight = jnp.where(inside, 1.0 / size, weight)
        base = base + jnp.where(place >= alone, pairs(length), 0)
        start = start + length
    rows = first_ref.shape[0]
    k = lax.broadcasted_iota(jnp.int32, (rows, 1), 0)
    part = jnp.where(k >= room, 1, 0) + jnp.where(k >= 2 * room, 1, 0) + jnp.where(k >= 3 * room, 1, 0)
    p = k - part * room
    lane = lax.broadcasted_iota(jnp.int32, (rows, total), 1)
    one = jnp.logical_and(jnp.logical_and(p >= begins, p < begins + count), part < 3)
    mate = p + jnp.sum(jnp.where(one, lane - begins, 0), axis=1, keepdims=True)
    there = jnp.sum(jnp.where(one, 1, 0), axis=1, keepdims=True) > 0
    two = jnp.logical_and(lane == mate, there)
    both = jnp.sum(jnp.where(jnp.logical_and(one, two), 1.0, 0.0), axis=1, keepdims=True)
    first_ref[...] = jnp.where(one, 1.0, 0.0).astype(jnp.bfloat16)
    second_ref[...] = jnp.where(two, 1.0, 0.0).astype(jnp.bfloat16)
    scale_ref[...] = (2.0 - both) * jnp.sum(jnp.where(one, jnp.broadcast_to(weight, one.shape), 0.0), axis=1, keepdims=True)
    order_ref[2 * seqs + 1] = room


def halves(values):
    high = values.astype(jnp.bfloat16)
    return high, (values - high.astype(jnp.float32)).astype(jnp.bfloat16)


def kernel(seqs, longest, tile, tiles, quarters, where_ref, *refs):
    h_refs, c_refs, out_ref = refs[:2], refs[2:4], refs[-10]
    order_ref, pick_ref, first_ref, second_ref, scale_ref, c_own, c_shared, h_own, h_shared = refs[-9:]
    step = pl.program_id(0)

    @pl.when(step == 0)
    def _():
        choose(where_ref, seqs, order_ref)
        select(where_ref, order_ref, seqs, longest, pick_ref, first_ref, second_ref, scale_ref)

    plan = order_ref[2 * seqs]

    def part_of(n, room):
        k = lax.broadcasted_iota(jnp.int32, (DEPTH, 1), 0) + n * DEPTH
        return jnp.where(k >= room, 1, 0) + jnp.where(k >= 2 * room, 1, 0)

    def shared(source, to, low_part, scale):
        for n in range(2):
            used = functools.reduce(jnp.logical_or, [plan == i for i in range(len(PLANS)) if PLANS[i][1] > n])

            @pl.when(used)
            def _(n=n):
                rows = pl.ds(n * DEPTH, DEPTH)
                one = lax.dot_general(first_ref[rows, :], source[...], PLAIN, preferred_element_type=jnp.float32)
                two = lax.dot_general(second_ref[rows, :], source[...], PLAIN, preferred_element_type=jnp.float32)
                value = one * two
                if scale:
                    value = value * scale_ref[rows, :]
                high, low = halves(value)
                is_low = part_of(n, order_ref[2 * seqs + 1]) == low_part
                to[rows, :] = jnp.where(is_low, low.astype(jnp.float32), high.astype(jnp.float32)).astype(jnp.bfloat16)

    def prepare_c(c_ref):
        rows = lax.dot_general(pick_ref[...], c_ref[...], PLAIN, preferred_element_type=jnp.float32)
        for j in range(seqs):
            size = jnp.full((1, 1), seqs * order_ref[j], jnp.int32).astype(jnp.float32)
            high, low = halves(rows[j * longest : (j + 1) * longest] * lax.rsqrt(size))
            c_own[j, :longest, :] = high
            c_own[j, longest:, :] = low
        shared(c_ref, c_shared, 2, True)

    def prepare_h(h_ref):
        rows = lax.dot_general(pick_ref[...], h_ref[...], PLAIN, preferred_element_type=jnp.float32)
        rows = rows.astype(jnp.bfloat16)
        for j in range(seqs):
            h_own[j, :longest, :] = rows[j * longest : (j + 1) * longest]
            h_own[j, longest:, :] = rows[j * longest : (j + 1) * longest]
        shared(h_ref, h_shared, 1, False)

    held = (None, None)
    for q, (h, c) in enumerate(quarters):
        if c != held[1]:
            pl.when(step == q * tiles)(functools.partial(prepare_c, c_refs[c]))
        if h != held[0]:
            pl.when(step == q * tiles)(functools.partial(prepare_h, h_refs[h]))
        held = (h, c)

    columns = pl.ds(pl.multiple_of(lax.rem(step, tiles) * tile, tile), tile)
    for n, (alone, dots) in enumerate(PLANS):

        @pl.when(plan == n)
        def _(alone=alone, dots=dots):
            fisher = None
            for j in range(alone):
                grad = lax.dot_general(h_own[j, :, columns], c_own[j], FIRST, preferred_element_type=jnp.float32)
                fisher = grad * grad if fisher is None else fisher + grad * grad
            if dots:
                depth = pl.ds(0, dots * DEPTH)
                fisher = fisher + lax.dot_general(
                    h_shared[depth, columns], c_shared[depth, :], FIRST, preferred_element_type=jnp.float32
                )
            out_ref[...] = fisher


def blocks(seqs, where, h, c, quarters, before, tile=896):
    total, half_h = h[0].shape
    half_c = c[0].shape[1]
    longest = total // 4
    tiles = half_h // tile

    def where_out(step, where):
        q = step // tiles
        hs = sum((q == n) * h for n, (h, _) in enumerate(quarters))
        cs = sum((q == n) * c for n, (_, c) in enumerate(quarters))
        return (where[0] ^ hs) * tiles + lax.rem(step, tiles), where[1] ^ cs

    whole = lambda a: pl.BlockSpec(a.shape, lambda step, where: (0, 0))
    args = [*h, *c]
    specs = [whole(a) for a in args]
    aliases = {}
    if before is not None:
        aliases = {1 + len(args): 0}
        args.append(before)
        specs.append(pl.BlockSpec(memory_space=pl.ANY))
    return pl.pallas_call(
        functools.partial(kernel, seqs, longest, tile, tiles, quarters),
        grid_spec=pltpu.PrefetchScalarGridSpec(
            num_scalar_prefetch=1,
            grid=(len(quarters) * tiles,),
            in_specs=specs,
            out_specs=pl.BlockSpec((tile, half_c), where_out),
            scratch_shapes=[
                pltpu.SMEM((2 * seqs + 2,), jnp.int32),
                pltpu.VMEM((seqs * longest, total), jnp.bfloat16),
                pltpu.VMEM((2 * DEPTH, total), jnp.bfloat16),
                pltpu.VMEM((2 * DEPTH, total), jnp.bfloat16),
                pltpu.VMEM((2 * DEPTH, 1), jnp.float32),
                pltpu.VMEM((seqs, 2 * longest, half_c), jnp.bfloat16),
                pltpu.VMEM((2 * DEPTH, half_c), jnp.bfloat16),
                pltpu.VMEM((seqs, 2 * longest, half_h), jnp.bfloat16),
                pltpu.VMEM((2 * DEPTH, half_h), jnp.bfloat16),
            ],
        ),
        out_shape=jax.ShapeDtypeStruct((2 * half_h, 2 * half_c), jnp.float32),
        input_output_aliases=aliases,
        compiler_params=pltpu.CompilerParams(vmem_limit_bytes=32 << 20),
        cost_estimate=pl.CostEstimate(
            flops=len(quarters) * half_h * half_c * 2 * 256 * seqs,
            bytes_accessed=len(quarters) * half_h * half_c * 4,
            transcendentals=0,
        ),
        name=f"fisher_{len(quarters)}",
    )(where, *args)


def fisher_long(lengths, rows_h, rows_c):
    total = rows_c.shape[0]
    seqs = lengths.shape[0]
    longest = total // 4
    ends = jnp.cumsum(lengths)
    starts = ends - lengths
    weights = 1.0 / lengths.astype(jnp.float32)
    fisher = jnp.zeros((rows_h.shape[1], rows_c.shape[1]), jnp.float32)
    for s in range(seqs):
        lower = jnp.minimum(starts[s], total - longest)
        piece_h = lax.dynamic_slice_in_dim(rows_h, lower, longest, 0)
        piece_c = lax.dynamic_slice_in_dim(rows_c, lower, longest, 0)
        places = lower + jnp.arange(longest, dtype=jnp.int32)
        keep = (places >= starts[s]) & (places < ends[s])
        piece_c = jnp.where(keep[:, None], piece_c, jnp.zeros_like(piece_c))
        grad = lax.dot_general(piece_h, piece_c, FIRST, preferred_element_type=jnp.float32)
        fisher = fisher + grad * grad * weights[s]
    return fisher / jnp.float32(seqs)


def shards(dp, tensor, hidden, cotangent, lengths):
    half_h, half_c = hidden.shape[1] // dp // 2, cotangent.shape[1] // 2
    if tensor != 2 or dp % 2 or dp * hidden.shape[0] > 128 or half_h % 896 or half_c % 128:
        rows_h = lax.all_to_all(hidden, "dp", split_axis=1, concat_axis=0, tiled=True)
        rows_c = lax.all_gather(cotangent, "dp", axis=0, tiled=True)
        return fisher_long(lengths, rows_h, rows_c)
    place = jnp.stack([lax.axis_index("tensor"), lax.rem(lax.axis_index("dp"), 2)]).astype(jnp.int32)
    where = jnp.concatenate([place, lengths])
    sent = pack(where, hidden, cotangent, dp)
    mine = lax.all_to_all(sent, "dp", split_axis=0, concat_axis=0, tiled=True)
    mine = mine.reshape(-1, half_h + half_c)
    mine_h, mine_c = mine[:, :half_h], mine[:, half_h:]
    other_h = lax.ppermute(mine_h, "tensor", [(0, 1), (1, 0)])
    other_c = lax.ppermute(mine_c, "dp", [(i, i ^ 1) for i in range(dp)])
    out = blocks(lengths.shape[0], where, [mine_h, mine_h], [mine_c, mine_c], ((0, 0),), None)
    rest = ((1, 0), (1, 1), (0, 1))
    return blocks(lengths.shape[0], where, [mine_h, other_h], [mine_c, other_c], rest, out)


def solution(mesh):
    return jax.shard_map(
        functools.partial(shards, mesh.shape["dp"], mesh.shape["tensor"]),
        mesh=mesh,
        in_specs=(P(("groups", "dp"), None), P(("groups", "dp"), "tensor"), P("groups")),
        out_specs=P(("groups", "dp"), "tensor"),
        check_vma=False,
    )
```

```python
import functools
import jax
import jax.numpy as jnp
from jax import lax
from jax.experimental import pallas as pl
from jax.experimental.pallas import tpu as pltpu
from jax.sharding import PartitionSpec as P

FIRST = (((0,), (0,)), ((), ()))
PLAIN = (((1,), (0,)), ((), ()))


def pack_kernel(h_ref, c_ref, out_ref):
    dp = out_ref.shape[0]
    half_h, half_c = h_ref.shape[1] // dp // 2, c_ref.shape[1] // 2
    core = lax.axis_index("tensor")
    for d in range(dp):
        at = pl.multiple_of((2 * d + core) * half_h, 128)
        out_ref[d, :, :half_h] = h_ref[:, pl.ds(at, half_h)]
        out_ref[d, :, half_h:] = c_ref[:, (d % 2) * half_c : (d % 2 + 1) * half_c]


def pack(hidden, cotangent, dp):
    rows = hidden.shape[0]
    half_h, half_c = hidden.shape[1] // dp // 2, cotangent.shape[1] // 2
    return pl.pallas_call(
        pack_kernel,
        in_specs=[pl.BlockSpec(memory_space=pltpu.VMEM)] * 2,
        out_specs=pl.BlockSpec(memory_space=pltpu.VMEM),
        out_shape=jax.ShapeDtypeStruct((dp, rows, half_h + half_c), hidden.dtype),
        compiler_params=pltpu.CompilerParams(vmem_limit_bytes=32 << 20),
        name="pack",
    )(hidden, cotangent)


def pairs(length):
    return lax.shift_right_logical(length * (length + 1), 1)


DEPTH = 256
PLANS = ((5, 1), (4, 2), (6, 1), (8, 0))


def choose(lengths_ref, seqs, order_ref):
    lengths = [lengths_ref[s] for s in range(seqs)]
    places = []
    for s in range(seqs):
        ahead = [
            jnp.where(lengths[r] >= lengths[s] if r < s else lengths[r] > lengths[s], 1, 0) for r in range(seqs) if r != s
        ]
        places.append(functools.reduce(jnp.add, ahead))
    ordered = []
    for j in range(seqs):
        ordered.append(functools.reduce(jnp.add, [jnp.where(places[s] == j, lengths[s], 0) for s in range(seqs)]))
        order_ref[j] = ordered[j]
        order_ref[seqs + j] = places[j]
    plan = jnp.int32(len(PLANS) - 1)
    for n in reversed(range(len(PLANS) - 1)):
        alone, dots = PLANS[n]
        number = functools.reduce(jnp.add, [pairs(length) for length in ordered[alone:]])
        plan = jnp.where(number <= DEPTH * dots // 3, n, plan)
    order_ref[2 * seqs] = plan


def select(lengths_ref, order_ref, seqs, longest, pick_ref, first_ref, second_ref, scale_ref):
    total = pick_ref.shape[1]
    plan = order_ref[2 * seqs]
    alone = functools.reduce(jnp.add, [jnp.where(plan == n, PLANS[n][0], 0) for n in range(len(PLANS))])
    room = functools.reduce(jnp.add, [jnp.where(plan == n, DEPTH * PLANS[n][1] // 3, 0) for n in range(len(PLANS))])
    row = lax.broadcasted_iota(jnp.int32, (longest, total), 0)
    token = lax.broadcasted_iota(jnp.int32, (longest, total), 1)
    at = lax.broadcasted_iota(jnp.int32, (1, total), 1)
    begins, count, weight = jnp.zeros_like(at), jnp.zeros_like(at), jnp.zeros(at.shape, jnp.float32)
    start, base = jnp.int32(0), jnp.int32(0)
    for s in range(seqs):
        length, place = lengths_ref[s], order_ref[seqs + s]
        take = jnp.logical_and(token == start + row, row < length)
        to = pl.multiple_of(place * longest, longest)
        pick_ref[pl.ds(to, longest), :] = jnp.where(take, 1.0, 0.0).astype(jnp.bfloat16)
        i = at - start
        inside = jnp.logical_and(jnp.logical_and(i >= 0, i < length), place >= alone)
        begins = jnp.where(inside, base + i * length - lax.shift_right_arithmetic(i * (i - 1), 1), begins)
        count = jnp.where(inside, length - i, count)
        size = jnp.full((1, 1), seqs * length, jnp.int32).astype(jnp.float32)
        weight = jnp.where(inside, 1.0 / size, weight)
        base = base + jnp.where(place >= alone, pairs(length), 0)
        start = start + length
    rows = first_ref.shape[0]
    k = lax.broadcasted_iota(jnp.int32, (rows, 1), 0)
    part = jnp.where(k >= room, 1, 0) + jnp.where(k >= 2 * room, 1, 0) + jnp.where(k >= 3 * room, 1, 0)
    p = k - part * room
    lane = lax.broadcasted_iota(jnp.int32, (rows, total), 1)
    one = jnp.logical_and(jnp.logical_and(p >= begins, p < begins + count), part < 3)
    mate = p + jnp.sum(jnp.where(one, lane - begins, 0), axis=1, keepdims=True)
    there = jnp.sum(jnp.where(one, 1, 0), axis=1, keepdims=True) > 0
    two = jnp.logical_and(lane == mate, there)
    both = jnp.sum(jnp.where(jnp.logical_and(one, two), 1.0, 0.0), axis=1, keepdims=True)
    first_ref[...] = jnp.where(one, 1.0, 0.0).astype(jnp.bfloat16)
    second_ref[...] = jnp.where(two, 1.0, 0.0).astype(jnp.bfloat16)
    scale_ref[...] = (2.0 - both) * jnp.sum(jnp.where(one, jnp.broadcast_to(weight, one.shape), 0.0), axis=1, keepdims=True)
    order_ref[2 * seqs + 1] = room


def halves(values):
    high = values.astype(jnp.bfloat16)
    return high, (values - high.astype(jnp.float32)).astype(jnp.bfloat16)


def kernel(seqs, longest, tile, tiles, quarters, lengths_ref, *refs):
    h_refs, c_refs, out_ref = refs[:2], refs[2:4], refs[-10]
    order_ref, pick_ref, first_ref, second_ref, scale_ref, c_own, c_shared, h_own, h_shared = refs[-9:]
    step = pl.program_id(0)

    @pl.when(step == 0)
    def _():
        choose(lengths_ref, seqs, order_ref)
        select(lengths_ref, order_ref, seqs, longest, pick_ref, first_ref, second_ref, scale_ref)

    plan = order_ref[2 * seqs]

    def part_of(n, room):
        k = lax.broadcasted_iota(jnp.int32, (DEPTH, 1), 0) + n * DEPTH
        return jnp.where(k >= room, 1, 0) + jnp.where(k >= 2 * room, 1, 0)

    def shared(source, to, low_part, scale):
        for n in range(2):
            used = functools.reduce(jnp.logical_or, [plan == i for i in range(len(PLANS)) if PLANS[i][1] > n])

            @pl.when(used)
            def _(n=n):
                rows = pl.ds(n * DEPTH, DEPTH)
                one = lax.dot_general(first_ref[rows, :], source[...], PLAIN, preferred_element_type=jnp.float32)
                two = lax.dot_general(second_ref[rows, :], source[...], PLAIN, preferred_element_type=jnp.float32)
                value = one * two
                if scale:
                    value = value * scale_ref[rows, :]
                high, low = halves(value)
                is_low = part_of(n, order_ref[2 * seqs + 1]) == low_part
                to[rows, :] = jnp.where(is_low, low.astype(jnp.float32), high.astype(jnp.float32)).astype(jnp.bfloat16)

    def prepare_c(c_ref):
        rows = lax.dot_general(pick_ref[...], c_ref[...], PLAIN, preferred_element_type=jnp.float32)
        for j in range(seqs):
            size = jnp.full((1, 1), seqs * order_ref[j], jnp.int32).astype(jnp.float32)
            high, low = halves(rows[j * longest : (j + 1) * longest] * lax.rsqrt(size))
            c_own[j, :longest, :] = high
            c_own[j, longest:, :] = low
        shared(c_ref, c_shared, 2, True)

    def prepare_h(h_ref):
        rows = lax.dot_general(pick_ref[...], h_ref[...], PLAIN, preferred_element_type=jnp.float32)
        rows = rows.astype(jnp.bfloat16)
        for j in range(seqs):
            h_own[j, :longest, :] = rows[j * longest : (j + 1) * longest]
            h_own[j, longest:, :] = rows[j * longest : (j + 1) * longest]
        shared(h_ref, h_shared, 1, False)

    held = (None, None)
    for q, (h, c) in enumerate(quarters):
        if c != held[1]:
            pl.when(step == q * tiles)(functools.partial(prepare_c, c_refs[c]))
        if h != held[0]:
            pl.when(step == q * tiles)(functools.partial(prepare_h, h_refs[h]))
        held = (h, c)

    columns = pl.ds(pl.multiple_of(lax.rem(step, tiles) * tile, tile), tile)
    for n, (alone, dots) in enumerate(PLANS):

        @pl.when(plan == n)
        def _(alone=alone, dots=dots):
            fisher = None
            for j in range(alone):
                grad = lax.dot_general(h_own[j, :, columns], c_own[j], FIRST, preferred_element_type=jnp.float32)
                fisher = grad * grad if fisher is None else fisher + grad * grad
            if dots:
                depth = pl.ds(0, dots * DEPTH)
                fisher = fisher + lax.dot_general(
                    h_shared[depth, columns], c_shared[depth, :], FIRST, preferred_element_type=jnp.float32
                )
            out_ref[...] = fisher


def blocks(lengths, h, c, quarters, before, tile):
    total, half_h = h[0].shape
    half_c = c[0].shape[1]
    seqs = lengths.shape[0]
    longest = total // 4
    tiles = half_h // tile

    def where_out(step, lengths):
        q = step // tiles
        hs = sum((q == n) * h for n, (h, _) in enumerate(quarters))
        cs = sum((q == n) * c for n, (_, c) in enumerate(quarters))
        core, side = lax.axis_index("tensor"), lax.rem(lax.axis_index("dp"), 2)
        return (core ^ hs) * tiles + lax.rem(step, tiles), side ^ cs

    whole = lambda a: pl.BlockSpec(a.shape, lambda step, lengths: (0, 0))
    args = [*h, *c]
    specs = [whole(a) for a in args]
    aliases = {}
    if before is not None:
        aliases = {1 + len(args): 0}
        args.append(before)
        specs.append(pl.BlockSpec(memory_space=pl.ANY))
    return pl.pallas_call(
        functools.partial(kernel, seqs, longest, tile, tiles, quarters),
        grid_spec=pltpu.PrefetchScalarGridSpec(
            num_scalar_prefetch=1,
            grid=(len(quarters) * tiles,),
            in_specs=specs,
            out_specs=pl.BlockSpec((tile, half_c), where_out),
            scratch_shapes=[
                pltpu.SMEM((2 * seqs + 2,), jnp.int32),
                pltpu.VMEM((seqs * longest, total), jnp.bfloat16),
                pltpu.VMEM((2 * DEPTH, total), jnp.bfloat16),
                pltpu.VMEM((2 * DEPTH, total), jnp.bfloat16),
                pltpu.VMEM((2 * DEPTH, 1), jnp.float32),
                pltpu.VMEM((seqs, 2 * longest, half_c), jnp.bfloat16),
                pltpu.VMEM((2 * DEPTH, half_c), jnp.bfloat16),
                pltpu.VMEM((seqs, 2 * longest, half_h), jnp.bfloat16),
                pltpu.VMEM((2 * DEPTH, half_h), jnp.bfloat16),
            ],
        ),
        out_shape=jax.ShapeDtypeStruct((2 * half_h, 2 * half_c), jnp.float32),
        input_output_aliases=aliases,
        compiler_params=pltpu.CompilerParams(vmem_limit_bytes=32 << 20),
        cost_estimate=pl.CostEstimate(
            flops=len(quarters) * half_h * half_c * 2 * 256 * seqs,
            bytes_accessed=len(quarters) * half_h * half_c * 4,
            transcendentals=0,
        ),
        name=f"fisher_{len(quarters)}",
    )(lengths, *args)


def fisher_long(lengths, rows_h, rows_c):
    total = rows_c.shape[0]
    seqs = lengths.shape[0]
    longest = total // 4
    ends = jnp.cumsum(lengths)
    starts = ends - lengths
    weights = 1.0 / lengths.astype(jnp.float32)
    fisher = jnp.zeros((rows_h.shape[1], rows_c.shape[1]), jnp.float32)
    for s in range(seqs):
        lower = jnp.minimum(starts[s], total - longest)
        piece_h = lax.dynamic_slice_in_dim(rows_h, lower, longest, 0)
        piece_c = lax.dynamic_slice_in_dim(rows_c, lower, longest, 0)
        places = lower + jnp.arange(longest, dtype=jnp.int32)
        keep = (places >= starts[s]) & (places < ends[s])
        piece_c = jnp.where(keep[:, None], piece_c, jnp.zeros_like(piece_c))
        grad = lax.dot_general(piece_h, piece_c, FIRST, preferred_element_type=jnp.float32)
        fisher = fisher + grad * grad * weights[s]
    return fisher / jnp.float32(seqs)


def shards(dp, tensor, hidden, cotangent, lengths):
    half_h, half_c = hidden.shape[1] // dp // 2, cotangent.shape[1] // 2
    if tensor != 2 or dp % 2 or dp * hidden.shape[0] > 128 or half_h % 896 or half_c % 128:
        rows_h = lax.all_to_all(hidden, "dp", split_axis=1, concat_axis=0, tiled=True)
        rows_c = lax.all_gather(cotangent, "dp", axis=0, tiled=True)
        return fisher_long(lengths, rows_h, rows_c)
    sent = pack(hidden, cotangent, dp)
    mine = lax.all_to_all(sent, "dp", split_axis=0, concat_axis=0, tiled=True)
    mine = mine.reshape(-1, half_h + half_c)
    mine_h, mine_c = mine[:, :half_h], mine[:, half_h:]
    other_h = lax.ppermute(mine_h, "tensor", [(0, 1), (1, 0)])
    other_c = lax.ppermute(mine_c, "dp", [(i, i ^ 1) for i in range(dp)])
    out = blocks(lengths, [mine_h, mine_h], [mine_c, mine_c], ((0, 0),), None, 256)
    rest = ((1, 0), (1, 1), (0, 1))
    return blocks(lengths, [mine_h, other_h], [mine_c, other_c], rest, out, 896)


def solution(mesh):
    return jax.shard_map(
        functools.partial(shards, mesh.shape["dp"], mesh.shape["tensor"]),
        mesh=mesh,
        in_specs=(P(("groups", "dp"), None), P(("groups", "dp"), "tensor"), P("groups")),
        out_specs=P(("groups", "dp"), "tensor"),
        check_vma=False,
    )
```

```python
import functools
import jax
import jax.numpy as jnp
from jax import lax
from jax.experimental import pallas as pl
from jax.experimental.pallas import tpu as pltpu
from jax.sharding import PartitionSpec as P

FIRST = (((0,), (0,)), ((), ()))
PLAIN = (((1,), (0,)), ((), ()))


def pack_kernel(h_ref, c_ref, out_ref):
    dp = out_ref.shape[0]
    half_h, half_c = h_ref.shape[1] // dp // 2, c_ref.shape[1] // 2
    core = lax.axis_index("tensor")
    for d in range(dp):
        at = pl.multiple_of((2 * d + core) * half_h, 128)
        out_ref[d, :, :half_h] = h_ref[:, pl.ds(at, half_h)]
        out_ref[d, :, half_h:] = c_ref[:, (d % 2) * half_c : (d % 2 + 1) * half_c]


def pack(hidden, cotangent, dp):
    rows = hidden.shape[0]
    half_h, half_c = hidden.shape[1] // dp // 2, cotangent.shape[1] // 2
    return pl.pallas_call(
        pack_kernel,
        in_specs=[pl.BlockSpec(memory_space=pltpu.VMEM)] * 2,
        out_specs=pl.BlockSpec(memory_space=pltpu.VMEM),
        out_shape=jax.ShapeDtypeStruct((dp, rows, half_h + half_c), hidden.dtype),
        compiler_params=pltpu.CompilerParams(vmem_limit_bytes=32 << 20),
        name="pack",
    )(hidden, cotangent)


def pairs(length):
    return lax.shift_right_logical(length * (length + 1), 1)


DEPTH = 256
ROOM = DEPTH // 3
PLANS = ((5, True), (6, True), (8, False))


def plan_kernel(seqs, longest, lengths_ref, plan_ref, pick_ref, scale_ref):
    total = pick_ref.shape[1]
    own = seqs * longest
    lengths = [lengths_ref[s] for s in range(seqs)]
    places = []
    for s in range(seqs):
        ahead = [
            jnp.where(lengths[r] >= lengths[s] if r < s else lengths[r] > lengths[s], 1, 0) for r in range(seqs) if r != s
        ]
        places.append(functools.reduce(jnp.add, ahead))
    ordered = [
        functools.reduce(jnp.add, [jnp.where(places[s] == j, lengths[s], 0) for s in range(seqs)]) for j in range(seqs)
    ]
    plan, alone = jnp.int32(len(PLANS) - 1), jnp.int32(seqs)
    for n in reversed(range(len(PLANS) - 1)):
        number = functools.reduce(jnp.add, [pairs(length) for length in ordered[PLANS[n][0] :]])
        plan = jnp.where(number <= ROOM, n, plan)
        alone = jnp.where(number <= ROOM, PLANS[n][0], alone)
    plan_ref[0] = plan

    row = lax.broadcasted_iota(jnp.int32, (longest, total), 0)
    token = lax.broadcasted_iota(jnp.int32, (longest, total), 1)
    at = lax.broadcasted_iota(jnp.int32, (1, total), 1)
    begins, count, weight = jnp.zeros_like(at), jnp.zeros_like(at), jnp.zeros(at.shape, jnp.float32)
    start, base = jnp.int32(0), jnp.int32(0)
    for s in range(seqs):
        length, place = lengths[s], places[s]
        take = jnp.logical_and(token == start + row, row < length)
        rows = pl.ds(pl.multiple_of(place * longest, longest), longest)
        pick_ref[rows, :] = jnp.where(take, 1.0, 0.0).astype(jnp.bfloat16)
        size = jnp.full((1, 1), seqs * length, jnp.int32).astype(jnp.float32)
        scale_ref[rows, :] = jnp.broadcast_to(lax.rsqrt(size), (longest, 1))
        i = at - start
        inside = jnp.logical_and(jnp.logical_and(i >= 0, i < length), place >= alone)
        begins = jnp.where(inside, base + i * length - lax.shift_right_arithmetic(i * (i - 1), 1), begins)
        count = jnp.where(inside, length - i, count)
        weight = jnp.where(inside, 1.0 / size, weight)
        base = base + jnp.where(place >= alone, pairs(length), 0)
        start = start + length
    k = lax.broadcasted_iota(jnp.int32, (DEPTH, 1), 0)
    p = k - jnp.where(k >= ROOM, ROOM, 0) - jnp.where(k >= 2 * ROOM, ROOM, 0)
    lane = lax.broadcasted_iota(jnp.int32, (DEPTH, total), 1)
    one = jnp.logical_and(jnp.logical_and(p >= begins, p < begins + count), k < 3 * ROOM)
    mate = p + jnp.sum(jnp.where(one, lane - begins, 0), axis=1, keepdims=True)
    there = jnp.sum(jnp.where(one, 1, 0), axis=1, keepdims=True) > 0
    two = jnp.logical_and(lane == mate, there)
    same = jnp.sum(jnp.where(jnp.logical_and(one, two), 1.0, 0.0), axis=1, keepdims=True)
    pick_ref[own : own + DEPTH, :] = jnp.where(one, 1.0, 0.0).astype(jnp.bfloat16)
    pick_ref[own + DEPTH :, :] = jnp.where(two, 1.0, 0.0).astype(jnp.bfloat16)
    weights = jnp.sum(jnp.where(one, jnp.broadcast_to(weight, one.shape), 0.0), axis=1, keepdims=True)
    scale_ref[own:, :] = (2.0 - same) * weights


def make_plan(lengths, total):
    seqs, longest = lengths.shape[0], total // 4
    return pl.pallas_call(
        functools.partial(plan_kernel, seqs, longest),
        in_specs=[pl.BlockSpec(memory_space=pltpu.SMEM)],
        out_specs=[
            pl.BlockSpec(memory_space=pltpu.SMEM),
            pl.BlockSpec(memory_space=pltpu.VMEM),
            pl.BlockSpec(memory_space=pltpu.VMEM),
        ],
        out_shape=[
            jax.ShapeDtypeStruct((1,), jnp.int32),
            jax.ShapeDtypeStruct((seqs * longest + 2 * DEPTH, total), jnp.bfloat16),
            jax.ShapeDtypeStruct((seqs * longest + DEPTH, 1), jnp.float32),
        ],
        compiler_params=pltpu.CompilerParams(vmem_limit_bytes=8 << 20),
        name="plan",
    )(lengths)


def kernel(seqs, longest, tile, tiles, quarters, plan_ref, pick_ref, scale_ref, *refs):
    h_refs, c_refs, out_ref = refs[:2], refs[2:4], refs[-5]
    c_own, c_shared, h_own, h_shared = refs[-4:]
    step = pl.program_id(0)
    plan = plan_ref[0]
    own = seqs * longest

    def rounded(values):
        return values.astype(jnp.bfloat16).astype(jnp.float32)

    def shared(source, to, low_part, scale):
        @pl.when(plan < len(PLANS) - 1)
        def _():
            one = lax.dot_general(pick_ref[own : own + DEPTH, :], source[...], PLAIN, preferred_element_type=jnp.float32)
            two = lax.dot_general(pick_ref[own + DEPTH :, :], source[...], PLAIN, preferred_element_type=jnp.float32)
            value = one * two
            if scale:
                value = value * scale_ref[own:, :]
            k = lax.broadcasted_iota(jnp.int32, (DEPTH, 1), 0)
            is_low = jnp.logical_and(k >= low_part * ROOM, k < (low_part + 1) * ROOM)
            to[...] = jnp.where(is_low, value - rounded(value), value).astype(jnp.bfloat16)

    def prepare_c(c_ref):
        rows = lax.dot_general(pick_ref[:own, :], c_ref[...], PLAIN, preferred_element_type=jnp.float32)
        rows = rows * scale_ref[:own, :]
        high = rows.astype(jnp.bfloat16)
        low = (rows - high.astype(jnp.float32)).astype(jnp.bfloat16)
        for j in range(seqs):
            c_own[j, :longest, :] = high[j * longest : (j + 1) * longest]
            c_own[j, longest:, :] = low[j * longest : (j + 1) * longest]
        shared(c_ref, c_shared, 2, True)

    def prepare_h(h_ref):
        rows = lax.dot_general(pick_ref[:own, :], h_ref[...], PLAIN, preferred_element_type=jnp.float32)
        rows = rows.astype(jnp.bfloat16)
        for j in range(seqs):
            h_own[j, :longest, :] = rows[j * longest : (j + 1) * longest]
            h_own[j, longest:, :] = rows[j * longest : (j + 1) * longest]
        shared(h_ref, h_shared, 1, False)

    held = (None, None)
    for q, (h, c) in enumerate(quarters):
        if c != held[1]:
            pl.when(step == q * tiles)(functools.partial(prepare_c, c_refs[c]))
        if h != held[0]:
            pl.when(step == q * tiles)(functools.partial(prepare_h, h_refs[h]))
        held = (h, c)

    columns = pl.ds(pl.multiple_of(lax.rem(step, tiles) * tile, tile), tile)
    for n, (alone, share) in enumerate(PLANS):

        @pl.when(plan == n)
        def _(alone=alone, share=share):
            fisher = None
            for j in range(alone):
                grad = lax.dot_general(h_own[j, :, columns], c_own[j], FIRST, preferred_element_type=jnp.float32)
                fisher = grad * grad if fisher is None else fisher + grad * grad
            if share:
                fisher = fisher + lax.dot_general(
                    h_shared[:, columns], c_shared[...], FIRST, preferred_element_type=jnp.float32
                )
            out_ref[...] = fisher


def blocks(seqs, plan, h, c, quarters, before, tile):
    total, half_h = h[0].shape
    half_c = c[0].shape[1]
    longest = total // 4
    tiles = half_h // tile

    def where_out(step, plan):
        q = step // tiles
        hs = sum((q == n) * h for n, (h, _) in enumerate(quarters))
        cs = sum((q == n) * c for n, (_, c) in enumerate(quarters))
        core, side = lax.axis_index("tensor"), lax.rem(lax.axis_index("dp"), 2)
        return (core ^ hs) * tiles + lax.rem(step, tiles), side ^ cs

    whole = lambda a: pl.BlockSpec(a.shape, lambda step, plan: (0, 0))
    args = [*plan[1:], *h, *c]
    specs = [whole(a) for a in args]
    aliases = {}
    if before is not None:
        aliases = {1 + len(args): 0}
        args.append(before)
        specs.append(pl.BlockSpec(memory_space=pl.ANY))
    return pl.pallas_call(
        functools.partial(kernel, seqs, longest, tile, tiles, quarters),
        grid_spec=pltpu.PrefetchScalarGridSpec(
            num_scalar_prefetch=1,
            grid=(len(quarters) * tiles,),
            in_specs=specs,
            out_specs=pl.BlockSpec((tile, half_c), where_out),
            scratch_shapes=[
                pltpu.VMEM((seqs, 2 * longest, half_c), jnp.bfloat16),
                pltpu.VMEM((DEPTH, half_c), jnp.bfloat16),
                pltpu.VMEM((seqs, 2 * longest, half_h), jnp.bfloat16),
                pltpu.VMEM((DEPTH, half_h), jnp.bfloat16),
            ],
        ),
        out_shape=jax.ShapeDtypeStruct((2 * half_h, 2 * half_c), jnp.float32),
        input_output_aliases=aliases,
        compiler_params=pltpu.CompilerParams(vmem_limit_bytes=32 << 20),
        cost_estimate=pl.CostEstimate(
            flops=len(quarters) * half_h * half_c * 2 * 256 * seqs,
            bytes_accessed=len(quarters) * half_h * half_c * 4,
            transcendentals=0,
        ),
        name=f"fisher_{len(quarters)}",
    )(plan[0], *args)


def fisher_long(lengths, rows_h, rows_c):
    total = rows_c.shape[0]
    seqs = lengths.shape[0]
    longest = total // 4
    ends = jnp.cumsum(lengths)
    starts = ends - lengths
    weights = 1.0 / lengths.astype(jnp.float32)
    fisher = jnp.zeros((rows_h.shape[1], rows_c.shape[1]), jnp.float32)
    for s in range(seqs):
        lower = jnp.minimum(starts[s], total - longest)
        piece_h = lax.dynamic_slice_in_dim(rows_h, lower, longest, 0)
        piece_c = lax.dynamic_slice_in_dim(rows_c, lower, longest, 0)
        places = lower + jnp.arange(longest, dtype=jnp.int32)
        keep = (places >= starts[s]) & (places < ends[s])
        piece_c = jnp.where(keep[:, None], piece_c, jnp.zeros_like(piece_c))
        grad = lax.dot_general(piece_h, piece_c, FIRST, preferred_element_type=jnp.float32)
        fisher = fisher + grad * grad * weights[s]
    return fisher / jnp.float32(seqs)


def shards(dp, tensor, hidden, cotangent, lengths):
    half_h, half_c = hidden.shape[1] // dp // 2, cotangent.shape[1] // 2
    if tensor != 2 or dp % 2 or dp * hidden.shape[0] > 128 or half_h % 896 or half_c % 128:
        rows_h = lax.all_to_all(hidden, "dp", split_axis=1, concat_axis=0, tiled=True)
        rows_c = lax.all_gather(cotangent, "dp", axis=0, tiled=True)
        return fisher_long(lengths, rows_h, rows_c)
    sent = pack(hidden, cotangent, dp)
    plan = make_plan(lengths, dp * hidden.shape[0])
    mine = lax.all_to_all(sent, "dp", split_axis=0, concat_axis=0, tiled=True)
    mine = mine.reshape(-1, half_h + half_c)
    mine_h, mine_c = mine[:, :half_h], mine[:, half_h:]
    other_h = lax.ppermute(mine_h, "tensor", [(0, 1), (1, 0)])
    other_c = lax.ppermute(mine_c, "dp", [(i, i ^ 1) for i in range(dp)])
    seqs = lengths.shape[0]
    out = blocks(seqs, plan, [mine_h, mine_h], [mine_c, mine_c], ((0, 0),), None, 896)
    rest = ((1, 0), (1, 1), (0, 1))
    return blocks(seqs, plan, [mine_h, other_h], [mine_c, other_c], rest, out, 896)


def solution(mesh):
    return jax.shard_map(
        functools.partial(shards, mesh.shape["dp"], mesh.shape["tensor"]),
        mesh=mesh,
        in_specs=(P(("groups", "dp"), None), P(("groups", "dp"), "tensor"), P("groups")),
        out_specs=P(("groups", "dp"), "tensor"),
        check_vma=False,
    )
```

```python
import functools
import jax
import jax.numpy as jnp
from jax import lax
from jax.experimental import pallas as pl
from jax.experimental.pallas import tpu as pltpu
from jax.sharding import PartitionSpec as P

FIRST = (((0,), (0,)), ((), ()))
PLAIN = (((1,), (0,)), ((), ()))


def pack_kernel(h_ref, c_ref, out_ref, held, sems):
    dp = out_ref.shape[0]
    half_h, half_c = h_ref.shape[1] // dp // 2, c_ref.shape[1] // 2
    core = lax.axis_index("tensor")
    arrive, leave = [], []
    for d in range(dp):
        at = pl.multiple_of((2 * d + core) * half_h, 128)
        features = pltpu.make_async_copy(h_ref.at[:, pl.ds(at, half_h)], held.at[d, :, pl.ds(0, half_h)], sems.at[0, d])
        columns = pltpu.make_async_copy(
            c_ref.at[:, pl.ds(d % 2 * half_c, half_c)], held.at[d, :, pl.ds(half_h, half_c)], sems.at[1, d]
        )
        arrive.append((features, columns))
        leave.append(pltpu.make_async_copy(held.at[d], out_ref.at[d], sems.at[2, d]))
        features.start()
        columns.start()
    for (features, columns), out in zip(arrive, leave):
        features.wait()
        columns.wait()
        out.start()
    for out in leave:
        out.wait()


def pack(hidden, cotangent, dp):
    rows = hidden.shape[0]
    half_h, half_c = hidden.shape[1] // dp // 2, cotangent.shape[1] // 2
    return pl.pallas_call(
        pack_kernel,
        in_specs=[pl.BlockSpec(memory_space=pltpu.HBM)] * 2,
        out_specs=pl.BlockSpec(memory_space=pltpu.HBM),
        out_shape=jax.ShapeDtypeStruct((dp, rows, half_h + half_c), hidden.dtype),
        scratch_shapes=[
            pltpu.VMEM((dp, rows, half_h + half_c), hidden.dtype),
            pltpu.SemaphoreType.DMA((3, dp)),
        ],
        name="pack",
    )(hidden, cotangent)


def pairs(length):
    return lax.shift_right_logical(length * (length + 1), 1)


DEPTH = 256
ROOM = DEPTH // 3
PLANS = ((5, True), (6, True), (8, False))


def plan_kernel(seqs, longest, lengths_ref, plan_ref, pick_ref, scale_ref):
    total = pick_ref.shape[1]
    own = seqs * longest
    lengths = [lengths_ref[s] for s in range(seqs)]
    places = []
    for s in range(seqs):
        ahead = [
            jnp.where(lengths[r] >= lengths[s] if r < s else lengths[r] > lengths[s], 1, 0) for r in range(seqs) if r != s
        ]
        places.append(functools.reduce(jnp.add, ahead))
    ordered = [
        functools.reduce(jnp.add, [jnp.where(places[s] == j, lengths[s], 0) for s in range(seqs)]) for j in range(seqs)
    ]
    plan, alone = jnp.int32(len(PLANS) - 1), jnp.int32(seqs)
    for n in reversed(range(len(PLANS) - 1)):
        number = functools.reduce(jnp.add, [pairs(length) for length in ordered[PLANS[n][0] :]])
        plan = jnp.where(number <= ROOM, n, plan)
        alone = jnp.where(number <= ROOM, PLANS[n][0], alone)
    plan_ref[0] = plan

    row = lax.broadcasted_iota(jnp.int32, (longest, total), 0)
    token = lax.broadcasted_iota(jnp.int32, (longest, total), 1)
    at = lax.broadcasted_iota(jnp.int32, (1, total), 1)
    begins, count, weight = jnp.zeros_like(at), jnp.zeros_like(at), jnp.zeros(at.shape, jnp.float32)
    start, base = jnp.int32(0), jnp.int32(0)
    for s in range(seqs):
        length, place = lengths[s], places[s]
        take = jnp.logical_and(token == start + row, row < length)
        rows = pl.ds(pl.multiple_of(place * longest, longest), longest)
        pick_ref[rows, :] = jnp.where(take, 1.0, 0.0).astype(jnp.bfloat16)
        size = jnp.full((1, 1), seqs * length, jnp.int32).astype(jnp.float32)
        scale_ref[rows, :] = jnp.broadcast_to(lax.rsqrt(size), (longest, 1))
        i = at - start
        inside = jnp.logical_and(jnp.logical_and(i >= 0, i < length), place >= alone)
        begins = jnp.where(inside, base + i * length - lax.shift_right_arithmetic(i * (i - 1), 1), begins)
        count = jnp.where(inside, length - i, count)
        weight = jnp.where(inside, 1.0 / size, weight)
        base = base + jnp.where(place >= alone, pairs(length), 0)
        start = start + length
    k = lax.broadcasted_iota(jnp.int32, (DEPTH, 1), 0)
    p = k - jnp.where(k >= ROOM, ROOM, 0) - jnp.where(k >= 2 * ROOM, ROOM, 0)
    lane = lax.broadcasted_iota(jnp.int32, (DEPTH, total), 1)
    one = jnp.logical_and(jnp.logical_and(p >= begins, p < begins + count), k < 3 * ROOM)
    mate = p + jnp.sum(jnp.where(one, lane - begins, 0), axis=1, keepdims=True)
    there = jnp.sum(jnp.where(one, 1, 0), axis=1, keepdims=True) > 0
    two = jnp.logical_and(lane == mate, there)
    same = jnp.sum(jnp.where(jnp.logical_and(one, two), 1.0, 0.0), axis=1, keepdims=True)
    pick_ref[own : own + DEPTH, :] = jnp.where(one, 1.0, 0.0).astype(jnp.bfloat16)
    pick_ref[own + DEPTH :, :] = jnp.where(two, 1.0, 0.0).astype(jnp.bfloat16)
    weights = jnp.sum(jnp.where(one, jnp.broadcast_to(weight, one.shape), 0.0), axis=1, keepdims=True)
    scale_ref[own:, :] = (2.0 - same) * weights


def make_plan(lengths, total):
    seqs, longest = lengths.shape[0], total // 4
    return pl.pallas_call(
        functools.partial(plan_kernel, seqs, longest),
        in_specs=[pl.BlockSpec(memory_space=pltpu.SMEM)],
        out_specs=[
            pl.BlockSpec(memory_space=pltpu.SMEM),
            pl.BlockSpec(memory_space=pltpu.VMEM),
            pl.BlockSpec(memory_space=pltpu.VMEM),
        ],
        out_shape=[
            jax.ShapeDtypeStruct((1,), jnp.int32),
            jax.ShapeDtypeStruct((seqs * longest + 2 * DEPTH, total), jnp.bfloat16),
            jax.ShapeDtypeStruct((seqs * longest + DEPTH, 1), jnp.float32),
        ],
        compiler_params=pltpu.CompilerParams(vmem_limit_bytes=8 << 20),
        name="plan",
    )(lengths)


def kernel(seqs, longest, tile, tiles, quarters, plan_ref, pick_ref, scale_ref, *refs):
    h_refs, c_refs, out_ref = refs[:2], refs[2:4], refs[-5]
    c_own, c_shared, h_own, h_shared = refs[-4:]
    step = pl.program_id(0)
    plan = plan_ref[0]
    own = seqs * longest

    def rounded(values):
        return values.astype(jnp.bfloat16).astype(jnp.float32)

    def shared(source, to, low_part, scale):
        @pl.when(plan < len(PLANS) - 1)
        def _():
            one = lax.dot_general(pick_ref[own : own + DEPTH, :], source[...], PLAIN, preferred_element_type=jnp.float32)
            two = lax.dot_general(pick_ref[own + DEPTH :, :], source[...], PLAIN, preferred_element_type=jnp.float32)
            value = one * two
            if scale:
                value = value * scale_ref[own:, :]
            k = lax.broadcasted_iota(jnp.int32, (DEPTH, 1), 0)
            is_low = jnp.logical_and(k >= low_part * ROOM, k < (low_part + 1) * ROOM)
            to[...] = jnp.where(is_low, value - rounded(value), value).astype(jnp.bfloat16)

    def prepare_c(c_ref):
        rows = lax.dot_general(pick_ref[:own, :], c_ref[...], PLAIN, preferred_element_type=jnp.float32)
        rows = rows * scale_ref[:own, :]
        high = rows.astype(jnp.bfloat16)
        low = (rows - high.astype(jnp.float32)).astype(jnp.bfloat16)
        for j in range(seqs):
            c_own[j, :longest, :] = high[j * longest : (j + 1) * longest]
            c_own[j, longest:, :] = low[j * longest : (j + 1) * longest]
        shared(c_ref, c_shared, 2, True)

    def prepare_h(h_ref):
        rows = lax.dot_general(pick_ref[:own, :], h_ref[...], PLAIN, preferred_element_type=jnp.float32)
        rows = rows.astype(jnp.bfloat16)
        for j in range(seqs):
            h_own[j, :longest, :] = rows[j * longest : (j + 1) * longest]
            h_own[j, longest:, :] = rows[j * longest : (j + 1) * longest]
        shared(h_ref, h_shared, 1, False)

    held = (None, None)
    for q, (h, c) in enumerate(quarters):
        if c != held[1]:
            pl.when(step == q * tiles)(functools.partial(prepare_c, c_refs[c]))
        if h != held[0]:
            pl.when(step == q * tiles)(functools.partial(prepare_h, h_refs[h]))
        held = (h, c)

    columns = pl.ds(pl.multiple_of(lax.rem(step, tiles) * tile, tile), tile)
    for n, (alone, share) in enumerate(PLANS):

        @pl.when(plan == n)
        def _(alone=alone, share=share):
            fisher = None
            for j in range(alone):
                grad = lax.dot_general(h_own[j, :, columns], c_own[j], FIRST, preferred_element_type=jnp.float32)
                fisher = grad * grad if fisher is None else fisher + grad * grad
            if share:
                fisher = fisher + lax.dot_general(
                    h_shared[:, columns], c_shared[...], FIRST, preferred_element_type=jnp.float32
                )
            out_ref[...] = fisher


def blocks(seqs, plan, h, c, quarters, before, tile):
    total, half_h = h[0].shape
    half_c = c[0].shape[1]
    longest = total // 4
    tiles = half_h // tile

    def where_out(step, plan):
        q = step // tiles
        hs = sum((q == n) * h for n, (h, _) in enumerate(quarters))
        cs = sum((q == n) * c for n, (_, c) in enumerate(quarters))
        core, side = lax.axis_index("tensor"), lax.rem(lax.axis_index("dp"), 2)
        return (core ^ hs) * tiles + lax.rem(step, tiles), side ^ cs

    whole = lambda a: pl.BlockSpec(a.shape, lambda step, plan: (0, 0))
    args = [*plan[1:], *h, *c]
    specs = [whole(a) for a in args]
    aliases = {}
    if before is not None:
        aliases = {1 + len(args): 0}
        args.append(before)
        specs.append(pl.BlockSpec(memory_space=pl.ANY))
    return pl.pallas_call(
        functools.partial(kernel, seqs, longest, tile, tiles, quarters),
        grid_spec=pltpu.PrefetchScalarGridSpec(
            num_scalar_prefetch=1,
            grid=(len(quarters) * tiles,),
            in_specs=specs,
            out_specs=pl.BlockSpec((tile, half_c), where_out),
            scratch_shapes=[
                pltpu.VMEM((seqs, 2 * longest, half_c), jnp.bfloat16),
                pltpu.VMEM((DEPTH, half_c), jnp.bfloat16),
                pltpu.VMEM((seqs, 2 * longest, half_h), jnp.bfloat16),
                pltpu.VMEM((DEPTH, half_h), jnp.bfloat16),
            ],
        ),
        out_shape=jax.ShapeDtypeStruct((2 * half_h, 2 * half_c), jnp.float32),
        input_output_aliases=aliases,
        compiler_params=pltpu.CompilerParams(vmem_limit_bytes=32 << 20),
        cost_estimate=pl.CostEstimate(
            flops=len(quarters) * half_h * half_c * 2 * 256 * seqs,
            bytes_accessed=len(quarters) * half_h * half_c * 4,
            transcendentals=0,
        ),
        name=f"fisher_{len(quarters)}",
    )(plan[0], *args)


def fisher_long(lengths, rows_h, rows_c):
    total = rows_c.shape[0]
    seqs = lengths.shape[0]
    longest = total // 4
    ends = jnp.cumsum(lengths)
    starts = ends - lengths
    weights = 1.0 / lengths.astype(jnp.float32)
    fisher = jnp.zeros((rows_h.shape[1], rows_c.shape[1]), jnp.float32)
    for s in range(seqs):
        lower = jnp.minimum(starts[s], total - longest)
        piece_h = lax.dynamic_slice_in_dim(rows_h, lower, longest, 0)
        piece_c = lax.dynamic_slice_in_dim(rows_c, lower, longest, 0)
        places = lower + jnp.arange(longest, dtype=jnp.int32)
        keep = (places >= starts[s]) & (places < ends[s])
        piece_c = jnp.where(keep[:, None], piece_c, jnp.zeros_like(piece_c))
        grad = lax.dot_general(piece_h, piece_c, FIRST, preferred_element_type=jnp.float32)
        fisher = fisher + grad * grad * weights[s]
    return fisher / jnp.float32(seqs)


def shards(dp, tensor, hidden, cotangent, lengths):
    half_h, half_c = hidden.shape[1] // dp // 2, cotangent.shape[1] // 2
    if tensor != 2 or dp % 2 or dp * hidden.shape[0] > 128 or half_h % 896 or half_c % 128:
        rows_h = lax.all_to_all(hidden, "dp", split_axis=1, concat_axis=0, tiled=True)
        rows_c = lax.all_gather(cotangent, "dp", axis=0, tiled=True)
        return fisher_long(lengths, rows_h, rows_c)
    sent = pack(hidden, cotangent, dp)
    plan = make_plan(lengths, dp * hidden.shape[0])
    mine = lax.all_to_all(sent, "dp", split_axis=0, concat_axis=0, tiled=True)
    mine = mine.reshape(-1, half_h + half_c)
    mine_h, mine_c = mine[:, :half_h], mine[:, half_h:]
    other_h = lax.ppermute(mine_h, "tensor", [(0, 1), (1, 0)])
    other_c = lax.ppermute(mine_c, "dp", [(i, i ^ 1) for i in range(dp)])
    seqs = lengths.shape[0]
    out = blocks(seqs, plan, [mine_h, mine_h], [mine_c, mine_c], ((0, 0),), None, 896)
    rest = ((1, 0), (1, 1), (0, 1))
    return blocks(seqs, plan, [mine_h, other_h], [mine_c, other_c], rest, out, 896)


def solution(mesh):
    return jax.shard_map(
        functools.partial(shards, mesh.shape["dp"], mesh.shape["tensor"]),
        mesh=mesh,
        in_specs=(P(("groups", "dp"), None), P(("groups", "dp"), "tensor"), P("groups")),
        out_specs=P(("groups", "dp"), "tensor"),
        check_vma=False,
    )
```

```python
import functools
import jax
import jax.numpy as jnp
from jax import lax
from jax.experimental import pallas as pl
from jax.experimental.pallas import tpu as pltpu
from jax.sharding import PartitionSpec as P

FIRST = (((0,), (0,)), ((), ()))
PLAIN = (((1,), (0,)), ((), ()))


def pack_kernel(h_ref, c_ref, out_ref, held, sems):
    dp = out_ref.shape[0]
    half_h, half_c = h_ref.shape[1] // dp // 2, c_ref.shape[1] // 2
    core = lax.axis_index("tensor")
    arrive, leave = [], []
    for d in range(dp):
        at = pl.multiple_of((2 * d + core) * half_h, 128)
        features = pltpu.make_async_copy(h_ref.at[:, pl.ds(at, half_h)], held.at[d, :, pl.ds(0, half_h)], sems.at[0, d])
        columns = pltpu.make_async_copy(
            c_ref.at[:, pl.ds(d % 2 * half_c, half_c)], held.at[d, :, pl.ds(half_h, half_c)], sems.at[1, d]
        )
        arrive.append((features, columns))
        leave.append(pltpu.make_async_copy(held.at[d], out_ref.at[d], sems.at[2, d]))
        features.start()
        columns.start()
    for (features, columns), out in zip(arrive, leave):
        features.wait()
        columns.wait()
        out.start()
    for out in leave:
        out.wait()


def pack(hidden, cotangent, dp):
    rows = hidden.shape[0]
    half_h, half_c = hidden.shape[1] // dp // 2, cotangent.shape[1] // 2
    return pl.pallas_call(
        pack_kernel,
        in_specs=[pl.BlockSpec(memory_space=pltpu.HBM)] * 2,
        out_specs=pl.BlockSpec(memory_space=pltpu.HBM),
        out_shape=jax.ShapeDtypeStruct((dp, rows, half_h + half_c), hidden.dtype),
        scratch_shapes=[
            pltpu.VMEM((dp, rows, half_h + half_c), hidden.dtype),
            pltpu.SemaphoreType.DMA((3, dp)),
        ],
        name="pack",
    )(hidden, cotangent)


def pairs(length):
    return lax.shift_right_logical(length * (length + 1), 1)


DEPTH = 256
ROOM = DEPTH // 3
EVEN, FIRST_ROWS = 80, 96
ODD = ROOM - EVEN
PLANS = ((5, True), (6, True), (8, False))


def plan_kernel(seqs, longest, lengths_ref, plan_ref, pick_ref, scale_ref):
    total = pick_ref.shape[1]
    own = seqs * longest
    lengths = [lengths_ref[s] for s in range(seqs)]
    places = []
    for s in range(seqs):
        ahead = [
            jnp.where(lengths[r] >= lengths[s] if r < s else lengths[r] > lengths[s], 1, 0) for r in range(seqs) if r != s
        ]
        places.append(functools.reduce(jnp.add, ahead))
    ordered = [
        functools.reduce(jnp.add, [jnp.where(places[s] == j, lengths[s], 0) for s in range(seqs)]) for j in range(seqs)
    ]
    plan, alone = jnp.int32(len(PLANS) - 1), jnp.int32(seqs)
    for n in reversed(range(len(PLANS) - 1)):
        number = functools.reduce(jnp.add, [pairs(length) for length in ordered[PLANS[n][0] :]])
        plan = jnp.where(number <= ROOM, n, plan)
        alone = jnp.where(number <= ROOM, PLANS[n][0], alone)
    plan_ref[0] = plan

    row = lax.broadcasted_iota(jnp.int32, (longest, total), 0)
    token = lax.broadcasted_iota(jnp.int32, (longest, total), 1)
    at = lax.broadcasted_iota(jnp.int32, (1, total), 1)
    begins, count, weight = jnp.zeros_like(at), jnp.zeros_like(at), jnp.zeros(at.shape, jnp.float32)
    start, base = jnp.int32(0), jnp.int32(0)
    for s in range(seqs):
        length, place = lengths[s], places[s]
        take = jnp.logical_and(token == start + row, row < length)
        rows = pl.ds(pl.multiple_of(place * longest, longest), longest)
        pick_ref[rows, :] = jnp.where(take, 1.0, 0.0).astype(jnp.bfloat16)
        size = jnp.full((1, 1), seqs * length, jnp.int32).astype(jnp.float32)
        scale_ref[rows, :] = jnp.broadcast_to(lax.rsqrt(size), (longest, 1))
        i = at - start
        inside = jnp.logical_and(jnp.logical_and(i >= 0, i < length), place >= alone)
        begins = jnp.where(inside, base + i * length - lax.shift_right_arithmetic(i * (i - 1), 1), begins)
        count = jnp.where(inside, length - i, count)
        weight = jnp.where(inside, 1.0 / size, weight)
        base = base + jnp.where(place >= alone, pairs(length), 0)
        start = start + length
    k = lax.broadcasted_iota(jnp.int32, (FIRST_ROWS, 1), 0)
    p = k - jnp.where(k >= ROOM, ODD, 0) - jnp.where(k >= ROOM + ODD, ODD, 0)
    lane = lax.broadcasted_iota(jnp.int32, (FIRST_ROWS, total), 1)
    one = jnp.logical_and(jnp.logical_and(p >= begins, p < begins + count), k < ROOM + 2 * ODD)
    mate = p + jnp.sum(jnp.where(one, lane - begins, 0), axis=1, keepdims=True)
    there = jnp.sum(jnp.where(one, 1, 0), axis=1, keepdims=True) > 0
    two = jnp.logical_and(lane == mate, there)
    same = jnp.sum(jnp.where(jnp.logical_and(one, two), 1.0, 0.0), axis=1, keepdims=True)
    pick_ref[own : own + FIRST_ROWS, :] = jnp.where(one, 1.0, 0.0).astype(jnp.bfloat16)
    pick_ref[own + FIRST_ROWS :, :] = jnp.where(two, 1.0, 0.0).astype(jnp.bfloat16)
    weights = jnp.sum(jnp.where(one, jnp.broadcast_to(weight, one.shape), 0.0), axis=1, keepdims=True)
    scale_ref[own:, :] = (2.0 - same) * weights


def make_plan(lengths, total):
    seqs, longest = lengths.shape[0], total // 4
    return pl.pallas_call(
        functools.partial(plan_kernel, seqs, longest),
        in_specs=[pl.BlockSpec(memory_space=pltpu.SMEM)],
        out_specs=[
            pl.BlockSpec(memory_space=pltpu.SMEM),
            pl.BlockSpec(memory_space=pltpu.VMEM),
            pl.BlockSpec(memory_space=pltpu.VMEM),
        ],
        out_shape=[
            jax.ShapeDtypeStruct((1,), jnp.int32),
            jax.ShapeDtypeStruct((seqs * longest + 2 * FIRST_ROWS, total), jnp.bfloat16),
            jax.ShapeDtypeStruct((seqs * longest + FIRST_ROWS, 1), jnp.float32),
        ],
        compiler_params=pltpu.CompilerParams(vmem_limit_bytes=8 << 20),
        name="plan",
    )(lengths)


def kernel(seqs, longest, tile, tiles, quarters, plan_ref, pick_ref, scale_ref, *refs):
    h_refs, c_refs, out_ref = refs[:2], refs[2:4], refs[-5]
    c_own, c_shared, h_own, h_shared = refs[-4:]
    step = pl.program_id(0)
    plan = plan_ref[0]
    own = seqs * longest

    def rounded(values):
        return values.astype(jnp.bfloat16).astype(jnp.float32)

    def shared(source, to, low_part, scale):
        @pl.when(plan < len(PLANS) - 1)
        def _():
            rows = pick_ref[own : own + FIRST_ROWS, :]
            one = lax.dot_general(rows, source[...], PLAIN, preferred_element_type=jnp.float32)
            rows = pick_ref[own + FIRST_ROWS :, :]
            two = lax.dot_general(rows, source[...], PLAIN, preferred_element_type=jnp.float32)
            value = one * two
            if scale:
                value = value * scale_ref[own:, :]
            low = value - rounded(value)
            k = lax.broadcasted_iota(jnp.int32, (FIRST_ROWS, 1), 0)
            is_low = jnp.logical_and(k >= EVEN + low_part * ODD, k < EVEN + (low_part + 1) * ODD)
            to[:FIRST_ROWS, :] = jnp.where(is_low, low, value).astype(jnp.bfloat16)
            for part in (1, 2):
                at = FIRST_ROWS + (part - 1) * EVEN
                to[at : at + EVEN, :] = (low if part == low_part else value)[:EVEN].astype(jnp.bfloat16)

    def alone(source, store):
        most = max(PLANS[n][0] for n in range(len(PLANS) - 1))
        for first, last in ((0, most), (most, seqs)):

            @pl.when(jnp.logical_or(first == 0, plan == len(PLANS) - 1))
            def _(first=first, last=last):
                inside = pl.ds(first * longest, (last - first) * longest)
                rows = lax.dot_general(pick_ref[inside, :], source[...], PLAIN, preferred_element_type=jnp.float32)
                store(first, last, rows, inside)

    def prepare_c(c_ref):
        def store(first, last, rows, inside):
            rows = rows * scale_ref[inside, :]
            high = rows.astype(jnp.bfloat16)
            low = (rows - high.astype(jnp.float32)).astype(jnp.bfloat16)
            for j in range(first, last):
                at = (j - first) * longest
                c_own[j, :longest, :] = high[at : at + longest]
                c_own[j, longest:, :] = low[at : at + longest]

        alone(c_ref, store)
        shared(c_ref, c_shared, 2, True)

    def prepare_h(h_ref):
        def store(first, last, rows, inside):
            rows = rows.astype(jnp.bfloat16)
            for j in range(first, last):
                at = (j - first) * longest
                h_own[j, :longest, :] = rows[at : at + longest]
                h_own[j, longest:, :] = rows[at : at + longest]

        alone(h_ref, store)
        shared(h_ref, h_shared, 1, False)

    held = (None, None)
    for q, (h, c) in enumerate(quarters):
        if c != held[1]:
            pl.when(step == q * tiles)(functools.partial(prepare_c, c_refs[c]))
        if h != held[0]:
            pl.when(step == q * tiles)(functools.partial(prepare_h, h_refs[h]))
        held = (h, c)

    columns = pl.ds(pl.multiple_of(lax.rem(step, tiles) * tile, tile), tile)
    for n, (number, share) in enumerate(PLANS):

        @pl.when(plan == n)
        def _(number=number, share=share):
            fisher = None
            for j in range(number):
                grad = lax.dot_general(h_own[j, :, columns], c_own[j], FIRST, preferred_element_type=jnp.float32)
                fisher = grad * grad if fisher is None else fisher + grad * grad
            if share:
                fisher = fisher + lax.dot_general(
                    h_shared[:, columns], c_shared[...], FIRST, preferred_element_type=jnp.float32
                )
            out_ref[...] = fisher


def blocks(seqs, plan, h, c, quarters, before, tile):
    total, half_h = h[0].shape
    half_c = c[0].shape[1]
    longest = total // 4
    tiles = half_h // tile

    def where_out(step, plan):
        q = step // tiles
        hs = sum((q == n) * h for n, (h, _) in enumerate(quarters))
        cs = sum((q == n) * c for n, (_, c) in enumerate(quarters))
        core, side = lax.axis_index("tensor"), lax.rem(lax.axis_index("dp"), 2)
        return (core ^ hs) * tiles + lax.rem(step, tiles), side ^ cs

    whole = lambda a: pl.BlockSpec(a.shape, lambda step, plan: (0, 0))
    args = [*plan[1:], *h, *c]
    specs = [whole(a) for a in args]
    aliases = {}
    if before is not None:
        aliases = {1 + len(args): 0}
        args.append(before)
        specs.append(pl.BlockSpec(memory_space=pl.ANY))
    return pl.pallas_call(
        functools.partial(kernel, seqs, longest, tile, tiles, quarters),
        grid_spec=pltpu.PrefetchScalarGridSpec(
            num_scalar_prefetch=1,
            grid=(len(quarters) * tiles,),
            in_specs=specs,
            out_specs=pl.BlockSpec((tile, half_c), where_out),
            scratch_shapes=[
                pltpu.VMEM((seqs, 2 * longest, half_c), jnp.bfloat16),
                pltpu.VMEM((DEPTH, half_c), jnp.bfloat16),
                pltpu.VMEM((seqs, 2 * longest, half_h), jnp.bfloat16),
                pltpu.VMEM((DEPTH, half_h), jnp.bfloat16),
            ],
        ),
        out_shape=jax.ShapeDtypeStruct((2 * half_h, 2 * half_c), jnp.float32),
        input_output_aliases=aliases,
        compiler_params=pltpu.CompilerParams(vmem_limit_bytes=32 << 20),
        cost_estimate=pl.CostEstimate(
            flops=len(quarters) * half_h * half_c * 2 * 256 * seqs,
            bytes_accessed=len(quarters) * half_h * half_c * 4,
            transcendentals=0,
        ),
        name=f"fisher_{len(quarters)}",
    )(plan[0], *args)


def fisher_long(lengths, rows_h, rows_c):
    total = rows_c.shape[0]
    seqs = lengths.shape[0]
    longest = total // 4
    ends = jnp.cumsum(lengths)
    starts = ends - lengths
    weights = 1.0 / lengths.astype(jnp.float32)
    fisher = jnp.zeros((rows_h.shape[1], rows_c.shape[1]), jnp.float32)
    for s in range(seqs):
        lower = jnp.minimum(starts[s], total - longest)
        piece_h = lax.dynamic_slice_in_dim(rows_h, lower, longest, 0)
        piece_c = lax.dynamic_slice_in_dim(rows_c, lower, longest, 0)
        places = lower + jnp.arange(longest, dtype=jnp.int32)
        keep = (places >= starts[s]) & (places < ends[s])
        piece_c = jnp.where(keep[:, None], piece_c, jnp.zeros_like(piece_c))
        grad = lax.dot_general(piece_h, piece_c, FIRST, preferred_element_type=jnp.float32)
        fisher = fisher + grad * grad * weights[s]
    return fisher / jnp.float32(seqs)


def shards(dp, tensor, hidden, cotangent, lengths):
    half_h, half_c = hidden.shape[1] // dp // 2, cotangent.shape[1] // 2
    if tensor != 2 or dp % 2 or lengths.shape[0] != PLANS[-1][0] or dp * hidden.shape[0] > 128 or half_h % 896 or half_c % 128:
        rows_h = lax.all_to_all(hidden, "dp", split_axis=1, concat_axis=0, tiled=True)
        rows_c = lax.all_gather(cotangent, "dp", axis=0, tiled=True)
        return fisher_long(lengths, rows_h, rows_c)
    sent = pack(hidden, cotangent, dp)
    plan = make_plan(lengths, dp * hidden.shape[0])
    mine = lax.all_to_all(sent, "dp", split_axis=0, concat_axis=0, tiled=True)
    mine = mine.reshape(-1, half_h + half_c)
    mine_h, mine_c = mine[:, :half_h], mine[:, half_h:]
    other_h = lax.ppermute(mine_h, "tensor", [(0, 1), (1, 0)])
    other_c = lax.ppermute(mine_c, "dp", [(i, i ^ 1) for i in range(dp)])
    seqs = lengths.shape[0]
    out = blocks(seqs, plan, [mine_h, mine_h], [mine_c, mine_c], ((0, 0),), None, 896)
    rest = ((1, 0), (1, 1), (0, 1))
    return blocks(seqs, plan, [mine_h, other_h], [mine_c, other_c], rest, out, 896)


def solution(mesh):
    return jax.shard_map(
        functools.partial(shards, mesh.shape["dp"], mesh.shape["tensor"]),
        mesh=mesh,
        in_specs=(P(("groups", "dp"), None), P(("groups", "dp"), "tensor"), P("groups")),
        out_specs=P(("groups", "dp"), "tensor"),
        check_vma=False,
    )
```

```python
import functools
import jax
import jax.numpy as jnp
from jax import lax
from jax.experimental import pallas as pl
from jax.experimental.pallas import tpu as pltpu
from jax.sharding import PartitionSpec as P

FIRST = (((0,), (0,)), ((), ()))
PLAIN = (((1,), (0,)), ((), ()))


def pack_kernel(h_ref, c_ref, out_ref, held, sems):
    dp = out_ref.shape[0]
    half_h, half_c = h_ref.shape[1] // dp // 2, c_ref.shape[1] // 2
    core = lax.axis_index("tensor")
    arrive, leave = [], []
    for d in range(dp):
        at = pl.multiple_of((2 * d + core) * half_h, 128)
        features = pltpu.make_async_copy(h_ref.at[:, pl.ds(at, half_h)], held.at[d, :, pl.ds(0, half_h)], sems.at[0, d])
        columns = pltpu.make_async_copy(
            c_ref.at[:, pl.ds(d % 2 * half_c, half_c)], held.at[d, :, pl.ds(half_h, half_c)], sems.at[1, d]
        )
        arrive.append((features, columns))
        leave.append(pltpu.make_async_copy(held.at[d], out_ref.at[d], sems.at[2, d]))
        features.start()
        columns.start()
    for (features, columns), out in zip(arrive, leave):
        features.wait()
        columns.wait()
        out.start()
    for out in leave:
        out.wait()


def pack(hidden, cotangent, dp):
    rows = hidden.shape[0]
    half_h, half_c = hidden.shape[1] // dp // 2, cotangent.shape[1] // 2
    return pl.pallas_call(
        pack_kernel,
        in_specs=[pl.BlockSpec(memory_space=pltpu.HBM)] * 2,
        out_specs=pl.BlockSpec(memory_space=pltpu.HBM),
        out_shape=jax.ShapeDtypeStruct((dp, rows, half_h + half_c), hidden.dtype),
        scratch_shapes=[
            pltpu.VMEM((dp, rows, half_h + half_c), hidden.dtype),
            pltpu.SemaphoreType.DMA((3, dp)),
        ],
        name="pack",
    )(hidden, cotangent)


def pairs(length):
    return lax.shift_right_logical(length * (length + 1), 1)


DEPTH = 256
ROOM = DEPTH // 3
EVEN, FIRST_ROWS = 80, 96
ODD = ROOM - EVEN
PLANS = ((5, True), (6, True), (8, False))


def plan_kernel(seqs, longest, lengths_ref, plan_ref, pick_ref, scale_ref):
    total = pick_ref.shape[1]
    own = seqs * longest
    lengths = [lengths_ref[s] for s in range(seqs)]
    places = []
    for s in range(seqs):
        ahead = [
            jnp.where(lengths[r] >= lengths[s] if r < s else lengths[r] > lengths[s], 1, 0) for r in range(seqs) if r != s
        ]
        places.append(functools.reduce(jnp.add, ahead))
    ordered = [
        functools.reduce(jnp.add, [jnp.where(places[s] == j, lengths[s], 0) for s in range(seqs)]) for j in range(seqs)
    ]
    plan, alone = jnp.int32(len(PLANS) - 1), jnp.int32(seqs)
    for n in reversed(range(len(PLANS) - 1)):
        number = functools.reduce(jnp.add, [pairs(length) for length in ordered[PLANS[n][0] :]])
        plan = jnp.where(number <= ROOM, n, plan)
        alone = jnp.where(number <= ROOM, PLANS[n][0], alone)
    plan_ref[0] = plan

    row = lax.broadcasted_iota(jnp.int32, (longest, total), 0)
    token = lax.broadcasted_iota(jnp.int32, (longest, total), 1)
    at = lax.broadcasted_iota(jnp.int32, (1, total), 1)
    begins, count, weight = jnp.zeros_like(at), jnp.zeros_like(at), jnp.zeros(at.shape, jnp.float32)
    start, base = jnp.int32(0), jnp.int32(0)
    for s in range(seqs):
        length, place = lengths[s], places[s]
        take = jnp.logical_and(token == start + row, row < length)
        rows = pl.ds(pl.multiple_of(place * longest, longest), longest)
        pick_ref[rows, :] = jnp.where(take, 1.0, 0.0).astype(jnp.bfloat16)
        size = jnp.full((1, 1), seqs * length, jnp.int32).astype(jnp.float32)
        scale_ref[rows, :] = jnp.broadcast_to(lax.rsqrt(size), (longest, 1))
        i = at - start
        inside = jnp.logical_and(jnp.logical_and(i >= 0, i < length), place >= alone)
        begins = jnp.where(inside, base + i * length - lax.shift_right_arithmetic(i * (i - 1), 1), begins)
        count = jnp.where(inside, length - i, count)
        weight = jnp.where(inside, 1.0 / size, weight)
        base = base + jnp.where(place >= alone, pairs(length), 0)
        start = start + length
    k = lax.broadcasted_iota(jnp.int32, (FIRST_ROWS, 1), 0)
    p = k - jnp.where(k >= ROOM, ODD, 0) - jnp.where(k >= ROOM + ODD, ODD, 0)
    lane = lax.broadcasted_iota(jnp.int32, (FIRST_ROWS, total), 1)
    one = jnp.logical_and(jnp.logical_and(p >= begins, p < begins + count), k < ROOM + 2 * ODD)
    mate = p + jnp.sum(jnp.where(one, lane - begins, 0), axis=1, keepdims=True)
    there = jnp.sum(jnp.where(one, 1, 0), axis=1, keepdims=True) > 0
    two = jnp.logical_and(lane == mate, there)
    same = jnp.sum(jnp.where(jnp.logical_and(one, two), 1.0, 0.0), axis=1, keepdims=True)
    pick_ref[own : own + FIRST_ROWS, :] = jnp.where(one, 1.0, 0.0).astype(jnp.bfloat16)
    pick_ref[own + FIRST_ROWS :, :] = jnp.where(two, 1.0, 0.0).astype(jnp.bfloat16)
    weights = jnp.sum(jnp.where(one, jnp.broadcast_to(weight, one.shape), 0.0), axis=1, keepdims=True)
    scale_ref[own:, :] = (2.0 - same) * weights


def make_plan(lengths, total):
    seqs, longest = lengths.shape[0], total // 4
    return pl.pallas_call(
        functools.partial(plan_kernel, seqs, longest),
        in_specs=[pl.BlockSpec(memory_space=pltpu.SMEM)],
        out_specs=[
            pl.BlockSpec(memory_space=pltpu.SMEM),
            pl.BlockSpec(memory_space=pltpu.VMEM),
            pl.BlockSpec(memory_space=pltpu.VMEM),
        ],
        out_shape=[
            jax.ShapeDtypeStruct((1,), jnp.int32),
            jax.ShapeDtypeStruct((seqs * longest + 2 * FIRST_ROWS, total), jnp.bfloat16),
            jax.ShapeDtypeStruct((seqs * longest + FIRST_ROWS, 1), jnp.float32),
        ],
        compiler_params=pltpu.CompilerParams(vmem_limit_bytes=8 << 20),
        name="plan",
    )(lengths)


def kernel(seqs, longest, tile, tiles, quarters, plan_ref, pick_ref, scale_ref, *refs):
    halves = 1 + max(max(h, c) for h, c in quarters)
    h_refs, c_refs, out_ref = refs[:halves], refs[halves : 2 * halves], refs[-5]
    c_own, c_shared, h_own, h_shared = refs[-4:]
    step = pl.program_id(0)
    plan = plan_ref[0]
    own = seqs * longest

    def rounded(values):
        return values.astype(jnp.bfloat16).astype(jnp.float32)

    def shared(source, to, low_part, scale):
        @pl.when(plan < len(PLANS) - 1)
        def _():
            rows = pick_ref[own : own + FIRST_ROWS, :]
            one = lax.dot_general(rows, source[...], PLAIN, preferred_element_type=jnp.float32)
            rows = pick_ref[own + FIRST_ROWS :, :]
            two = lax.dot_general(rows, source[...], PLAIN, preferred_element_type=jnp.float32)
            value = one * two
            if scale:
                value = value * scale_ref[own:, :]
            low = value - rounded(value)
            k = lax.broadcasted_iota(jnp.int32, (FIRST_ROWS, 1), 0)
            is_low = jnp.logical_and(k >= EVEN + low_part * ODD, k < EVEN + (low_part + 1) * ODD)
            to[:FIRST_ROWS, :] = jnp.where(is_low, low, value).astype(jnp.bfloat16)
            for part in (1, 2):
                at = FIRST_ROWS + (part - 1) * EVEN
                to[at : at + EVEN, :] = (low if part == low_part else value)[:EVEN].astype(jnp.bfloat16)

    def alone(source, store):
        most = max(PLANS[n][0] for n in range(len(PLANS) - 1))
        for first, last in ((0, most), (most, seqs)):

            @pl.when(jnp.logical_or(first == 0, plan == len(PLANS) - 1))
            def _(first=first, last=last):
                inside = pl.ds(first * longest, (last - first) * longest)
                rows = lax.dot_general(pick_ref[inside, :], source[...], PLAIN, preferred_element_type=jnp.float32)
                store(first, last, rows, inside)

    def prepare_c(c_ref):
        def store(first, last, rows, inside):
            rows = rows * scale_ref[inside, :]
            high = rows.astype(jnp.bfloat16)
            low = (rows - high.astype(jnp.float32)).astype(jnp.bfloat16)
            for j in range(first, last):
                at = (j - first) * longest
                c_own[j, :longest, :] = high[at : at + longest]
                c_own[j, longest:, :] = low[at : at + longest]

        alone(c_ref, store)
        shared(c_ref, c_shared, 2, True)

    def prepare_h(h_ref):
        def store(first, last, rows, inside):
            rows = rows.astype(jnp.bfloat16)
            for j in range(first, last):
                at = (j - first) * longest
                h_own[j, :longest, :] = rows[at : at + longest]
                h_own[j, longest:, :] = rows[at : at + longest]

        alone(h_ref, store)
        shared(h_ref, h_shared, 1, False)

    held = (None, None)
    for q, (h, c) in enumerate(quarters):
        if c != held[1]:
            pl.when(step == q * tiles)(functools.partial(prepare_c, c_refs[c]))
        if h != held[0]:
            pl.when(step == q * tiles)(functools.partial(prepare_h, h_refs[h]))
        held = (h, c)

    columns = pl.ds(pl.multiple_of(lax.rem(step, tiles) * tile, tile), tile)
    for n, (number, share) in enumerate(PLANS):

        @pl.when(plan == n)
        def _(number=number, share=share):
            fisher = None
            for j in range(number):
                grad = lax.dot_general(h_own[j, :, columns], c_own[j], FIRST, preferred_element_type=jnp.float32)
                fisher = grad * grad if fisher is None else fisher + grad * grad
            if share:
                fisher = fisher + lax.dot_general(
                    h_shared[:, columns], c_shared[...], FIRST, preferred_element_type=jnp.float32
                )
            out_ref[...] = fisher


def blocks(seqs, plan, h, c, quarters, before, tile):
    total, half_h = h[0].shape
    half_c = c[0].shape[1]
    longest = total // 4
    tiles = half_h // tile

    def where_out(step, plan):
        q = step // tiles
        hs = sum((q == n) * h for n, (h, _) in enumerate(quarters))
        cs = sum((q == n) * c for n, (_, c) in enumerate(quarters))
        core, side = lax.axis_index("tensor"), lax.rem(lax.axis_index("dp"), 2)
        return (core ^ hs) * tiles + lax.rem(step, tiles), side ^ cs

    whole = lambda a: pl.BlockSpec(a.shape, lambda step, plan: (0, 0))
    args = [*plan[1:], *h, *c]
    specs = [whole(a) for a in args]
    aliases = {}
    if before is not None:
        aliases = {1 + len(args): 0}
        args.append(before)
        specs.append(pl.BlockSpec(memory_space=pl.ANY))
    return pl.pallas_call(
        functools.partial(kernel, seqs, longest, tile, tiles, quarters),
        grid_spec=pltpu.PrefetchScalarGridSpec(
            num_scalar_prefetch=1,
            grid=(len(quarters) * tiles,),
            in_specs=specs,
            out_specs=pl.BlockSpec((tile, half_c), where_out),
            scratch_shapes=[
                pltpu.VMEM((seqs, 2 * longest, half_c), jnp.bfloat16),
                pltpu.VMEM((DEPTH, half_c), jnp.bfloat16),
                pltpu.VMEM((seqs, 2 * longest, half_h), jnp.bfloat16),
                pltpu.VMEM((DEPTH, half_h), jnp.bfloat16),
            ],
        ),
        out_shape=jax.ShapeDtypeStruct((2 * half_h, 2 * half_c), jnp.float32),
        input_output_aliases=aliases,
        compiler_params=pltpu.CompilerParams(vmem_limit_bytes=32 << 20),
        cost_estimate=pl.CostEstimate(
            flops=len(quarters) * half_h * half_c * 2 * 256 * seqs,
            bytes_accessed=len(quarters) * half_h * half_c * 4,
            transcendentals=0,
        ),
        name=f"fisher_{len(quarters)}",
    )(plan[0], *args)


def fisher_long(lengths, rows_h, rows_c):
    total = rows_c.shape[0]
    seqs = lengths.shape[0]
    longest = total // 4
    ends = jnp.cumsum(lengths)
    starts = ends - lengths
    weights = 1.0 / lengths.astype(jnp.float32)
    fisher = jnp.zeros((rows_h.shape[1], rows_c.shape[1]), jnp.float32)
    for s in range(seqs):
        lower = jnp.minimum(starts[s], total - longest)
        piece_h = lax.dynamic_slice_in_dim(rows_h, lower, longest, 0)
        piece_c = lax.dynamic_slice_in_dim(rows_c, lower, longest, 0)
        places = lower + jnp.arange(longest, dtype=jnp.int32)
        keep = (places >= starts[s]) & (places < ends[s])
        piece_c = jnp.where(keep[:, None], piece_c, jnp.zeros_like(piece_c))
        grad = lax.dot_general(piece_h, piece_c, FIRST, preferred_element_type=jnp.float32)
        fisher = fisher + grad * grad * weights[s]
    return fisher / jnp.float32(seqs)


def shards(dp, tensor, hidden, cotangent, lengths):
    half_h, half_c = hidden.shape[1] // dp // 2, cotangent.shape[1] // 2
    if tensor != 2 or dp % 2 or lengths.shape[0] != PLANS[-1][0] or dp * hidden.shape[0] > 128 or half_h % 896 or half_c % 128:
        rows_h = lax.all_to_all(hidden, "dp", split_axis=1, concat_axis=0, tiled=True)
        rows_c = lax.all_gather(cotangent, "dp", axis=0, tiled=True)
        return fisher_long(lengths, rows_h, rows_c)
    sent = pack(hidden, cotangent, dp)
    plan = make_plan(lengths, dp * hidden.shape[0])
    mine = lax.all_to_all(sent, "dp", split_axis=0, concat_axis=0, tiled=True)
    mine = mine.reshape(-1, half_h + half_c)
    mine_h, mine_c = mine[:, :half_h], mine[:, half_h:]
    other_h = lax.ppermute(mine_h, "tensor", [(0, 1), (1, 0)])
    other_c = lax.ppermute(mine_c, "dp", [(i, i ^ 1) for i in range(dp)])
    seqs = lengths.shape[0]
    out = blocks(seqs, plan, [mine_h], [mine_c], ((0, 0),), None, 896)
    rest = ((1, 0), (1, 1), (0, 1))
    return blocks(seqs, plan, [mine_h, other_h], [mine_c, other_c], rest, out, 896)


def solution(mesh):
    return jax.shard_map(
        functools.partial(shards, mesh.shape["dp"], mesh.shape["tensor"]),
        mesh=mesh,
        in_specs=(P(("groups", "dp"), None), P(("groups", "dp"), "tensor"), P("groups")),
        out_specs=P(("groups", "dp"), "tensor"),
        check_vma=False,
    )
```
